128 devices in a mesh: seq: 32 (over z, y, core), sub: 4 (over x).
Axes of the slice: x: 4, y: 4, z: 4, core: 2. Of those that a mesh axis runs over, the one named last changes fastest.
Arguments:
- queries: bfloat16 [512, 8192], P(('seq', 'sub')), may hold values from -32 to 32, as said below
- query_positions: int32 [512], P(('seq', 'sub')), may hold values from 3584 to 4095
- keys: bfloat16 [524288, 512], P(('seq', 'sub')), may hold values from -8 to 8, as said below
- cache_values: bfloat16 [524288, 512], P(('seq', 'sub')), may hold values from -6 to 6
- cache_length: int32 [1], replicated, may hold values from 262145 to 524288
Outputs:
- scores: float32 [4, 524288], P(None, ('seq', 'sub'))
The draws below stay inside these ranges and needn't reach their ends.
Inputs may be any that keep to these rules, and one draw needn't show every extreme that they name: `queries`: custom draw; entries bounded. `keys`: custom draw; entries bounded.
All inputs are finite; a program needn't handle non-finite values.
Results may differ from the reference program's by a relative error of at most 0.00077.
Values sent between devices are 32-bit elements; how exact they have to be, the bound alone decides.
No kernel may reach another device: no remote copies, remote signals or barrier semaphores. Data moves between devices by JAX's collectives and lax.ppermute only.
A program may use at most 128 MiB of HBM per device.

```python
import math
import jax
import jax.numpy as jnp
from jax import lax

H = 64
KVH = 4
HD = 128
QN = 512
GROUP = 16
POSITIONS = 524288


def draw_keys(key, part):
    key = jax.random.fold_in(key, 11)
    first, second = jax.random.split(key, 2)
    scales = jnp.exp(jax.random.uniform(first, (KVH, HD), jnp.float32, jnp.log(0.5), jnp.log(2.0)))
    base = jnp.clip(jax.random.normal(second, (POSITIONS, KVH, HD), jnp.float32), -3.0, 3.0) * scales
    return jnp.clip(base, -8.0, 8.0).reshape(POSITIONS, KVH * HD).astype(jnp.bfloat16)


def draw_queries(key, part):
    key = jax.random.fold_in(key, 23)
    first = jax.random.fold_in(key, 0)
    second = jax.random.fold_in(key, 1)
    fourth = jax.random.fold_in(key, 3)
    fifth = jax.random.fold_in(key, 4)
    counts = jax.random.randint(second, (QN, H, HD), -7, 8).astype(jnp.float32)
    signs = (2 * jax.random.randint(fifth, (KVH, HD, HD), 0, 2) - 1).astype(jnp.float32)
    signs = jnp.repeat(signs, GROUP, axis=0)
    coupled = jnp.einsum('ihe,hed->ihd', counts, signs, precision=lax.Precision.HIGHEST) + 12.0 * counts
    unit_noise = coupled * (1.0 / math.sqrt(18.667 * (HD + 144)))
    scales = jnp.exp(jax.random.uniform(first, (H, HD), jnp.float32, jnp.log(0.7), jnp.log(3.0)))
    offset = jnp.clip(jax.random.normal(fourth, (H, HD), jnp.float32), -3.0, 3.0)
    values = jnp.clip(unit_noise * scales[None] + offset[None], -32.0, 32.0)
    return values.reshape(QN, H * HD).astype(jnp.bfloat16)


def place_ends(values, own_key, least, top_value):
    extent = values.shape
    spot = [jax.random.randint(jax.random.fold_in(own_key, axis), (), 0, extent[axis]) for axis in range(len(extent))]
    values = values.at[tuple(spot)].set(least)
    longest = extent.index(max(extent))
    spot[longest] = (spot[longest] + 1) % extent[longest]
    return values.at[tuple(spot)].set(top_value)


def shard_levels(stream_key, shape, cuts, smallest, high):
    gain, own = 1.0, jax.random.fold_in(stream_key, 6)
    for dim, shards_of in cuts:
        heights = jnp.exp(jax.random.uniform(jax.random.fold_in(own, dim), (shards_of,), jnp.float32, smallest / len(cuts), high / len(cuts)))
        gain = gain * jnp.repeat(heights, shape[dim] // shards_of).reshape([-1 if axis == dim else 1 for axis in range(len(shape))])
    return gain


def normal_values(own_key, dims, scale, bound, cuts=(), held_as=jnp.bfloat16):
    entries = jax.random.normal(own_key, dims, jnp.float32) * scale
    if len(cuts) > 0:
        entries = shard_levels(own_key, dims, cuts, -0.22, 0.18) * entries
    return jnp.clip(entries, min=-bound, max=bound).astype(held_as)


def setup_inputs(seed: int = 0) -> dict:
    seeds = jax.random.split(jax.random.key(seed), 6)
    queries = draw_queries(jax.random.fold_in(seeds[5], 71), 0)
    query_positions = place_ends(jax.random.randint(seeds[1], (QN,), 7 * QN, 8 * QN), jax.random.fold_in(seeds[1], 1), 7 * QN, (8 * QN) - 1).astype(jnp.int32)
    keys = draw_keys(jax.random.fold_in(seeds[5], 71), 0)
    cache_values = normal_values(seeds[3], (POSITIONS, KVH * HD), 1.0, 6.0, ((0, 128),))
    cache_length = jax.random.randint(seeds[4], (1,), POSITIONS // 2 + 1, POSITIONS + 1).astype(jnp.int32)
    return {"queries": queries, "query_positions": query_positions, "keys": keys, "cache_values": cache_values, "cache_length": cache_length}


def rotate_rows(queries, positions):
    count = queries.shape[0]
    values = queries.astype(jnp.float32).reshape(count, H, HD)
    half = HD // 2
    freqs = jnp.exp(-jnp.arange(half, dtype=jnp.float32) * (2.0 * math.log(1000000.0) / HD))
    angle = positions.astype(jnp.float32)[:, None] * freqs[None, :]
    cosine = jnp.concatenate([jnp.cos(angle), jnp.cos(angle)], axis=1)[:, None, :]
    sine = jnp.concatenate([jnp.sin(angle), jnp.sin(angle)], axis=1)[:, None, :]
    turned = jnp.concatenate([-values[:, :, half:], values[:, :, :half]], axis=2)
    return values * cosine + turned * sine

def block_logits(block, mean, sigma_cat):
    pieces = []
    for group in range(KVH):
        keyblk = block[:, group * HD:(group + 1) * HD]
        mixed = jnp.dot(keyblk, sigma_cat[group], preferred_element_type=jnp.float32)
        mixed = mixed.reshape(block.shape[0], GROUP, HD)
        inner = mean.reshape(KVH, GROUP, HD)[group][None] + mixed * (0.5 / math.sqrt(HD))
        keyf = keyblk.astype(jnp.float32)
        pieces.append(lax.optimization_barrier(jnp.sum(keyf[:, None, :] * inner, axis=2)).T / math.sqrt(HD))
    return jnp.concatenate(pieces, axis=0)

def reference(queries, query_positions, keys, cache_values, cache_length):
    rotated = rotate_rows(queries, query_positions)
    mean = lax.optimization_barrier(jnp.sum(rotated, axis=0)) / QN
    second = jnp.einsum('ihd,ihe->hde', rotated, rotated, precision=lax.Precision.HIGHEST) / QN
    sigma = (second - mean[:, :, None] * mean[:, None, :]).astype(jnp.bfloat16)
    sigma_cat = sigma.reshape(KVH, GROUP, HD, HD).transpose(0, 2, 1, 3).reshape(KVH, HD, GROUP * HD)
    width = math.gcd(POSITIONS, 4096)
    blocks = keys.reshape(POSITIONS // width, width, KVH * HD)
    logit = lax.map(lambda block: block_logits(block, mean, sigma_cat), blocks)
    logit = logit.transpose(1, 0, 2).reshape(H, POSITIONS)
    live = (jnp.arange(POSITIONS, dtype=jnp.int32) < cache_length[0])[None, :]
    peak = lax.optimization_barrier(jnp.max(jnp.where(live, logit, jnp.float32(-1e+30)), axis=1))
    weights = jnp.where(live, jnp.exp(jnp.where(live, logit - peak[:, None], 0.0)), 0.0)
    total = lax.optimization_barrier(jnp.sum(weights, axis=1))
    prob = weights / total[:, None]
    vals = cache_values.reshape(POSITIONS, KVH, HD).astype(jnp.float32)
    vnorm = jnp.sqrt(lax.optimization_barrier(jnp.mean(vals * vals, axis=2))).T
    summed = lax.optimization_barrier(jnp.sum(prob.reshape(KVH, GROUP, POSITIONS), axis=1))
    return summed * (POSITIONS / GROUP) * vnorm
```

```python
import math

import jax
import jax.numpy as jnp
from jax import lax
from jax.experimental import pallas as pl
from jax.experimental.pallas import tpu as pltpu
from jax.sharding import Mesh
from jax.sharding import PartitionSpec as P

H = 64
KVH = 4
HD = 128
QN = 512
GROUP = H // KVH
HALF = HD // 2
AXES = ("z", "y", "c", "x")
NZ, NY, NC, NX = 4, 4, 2, 4
OWNERS = NZ * NY
PLANES = OWNERS * NC
HP = H // PLANES
PACK = HALF + 8
OWN_HEADS = H // NC
OWN_GROUPS = KVH // NC
F32 = jnp.float32
BF16 = jnp.bfloat16
VMEM_LIMIT = 56 * 2**20


def iota(shape, dim):
    return lax.broadcasted_iota(jnp.int32, shape, dim)


def rotate_kernel(q_ref, cos_ref, sin_ref, out_ref):
    cos, sin = cos_ref[...], sin_ref[...]
    for plane in range(PLANES):
        zy, core = divmod(plane, NC)
        head = core * OWN_HEADS + zy * HP
        rows = [q_ref[:, (head + i) * HD : (head + i + 1) * HD].astype(F32) for i in range(HP)]
        v = jnp.concatenate(rows, axis=0)
        r = v * cos + pltpu.roll(v, HALF, 1) * sin
        for x in range(NX):
            out_ref[plane * NX + x] = r


def stats_kernel(r_ref, out_ref):
    per = r_ref.shape[1] // HP
    rows = r_ref.shape[0] * r_ref.shape[1]
    x = r_ref[...].reshape(rows, HD)
    sub = lax.rem(iota((rows, HD), 0), r_ref.shape[1]) // per
    row_h, lane_h = iota((HALF, HD), 0), iota((HALF, HD), 1)
    eye = iota((HD, HD), 0) == iota((HD, HD), 1)
    for i in range(HP):
        xi = jnp.where(sub == i, x, 0.0)
        second = lax.dot_general(
            xi, x, (((0,), (0,)), ((), ())), precision=lax.Precision.HIGHEST, preferred_element_type=F32
        )
        mean = jnp.sum(xi, axis=0, keepdims=True) * (1.0 / QN)
        mean_col = jnp.sum(jnp.where(eye, mean, 0.0), axis=1, keepdims=True)
        sigma = second * (1.0 / QN) - mean_col * mean
        diag = jnp.sum(jnp.where(eye, sigma, 0.0), axis=0, keepdims=True)
        packed = jnp.where(row_h < lane_h, sigma[:HALF], pltpu.roll(sigma[HALF:], HALF, 1))
        tail = jnp.concatenate([mean, diag, jnp.zeros((6, HD), F32)], axis=0)
        for o in range(OWNERS):
            out_ref[o, i * PACK : i * PACK + HALF, :] = packed
            out_ref[o, i * PACK + HALF : (i + 1) * PACK, :] = tail


def prep_kernel(k_ref, v_ref, kt_ref, vn_ref):
    kt_ref[...] = k_ref[...].T
    ones = jnp.ones((8, HD), BF16)
    nt = (((1,), (1,)), ((), ()))
    for g in range(KVH):
        v = v_ref[:, g * HD : (g + 1) * HD].astype(F32)
        sq = v * v
        hi = sq.astype(BF16)
        lo = (sq - hi.astype(F32)).astype(BF16)
        s = lax.dot_general(ones, hi, nt, preferred_element_type=F32)
        s = s + lax.dot_general(ones, lo, nt, preferred_element_type=F32)
        vn_ref[g : g + 1, :] = jnp.sqrt(s[:1] * (1.0 / HD))


def unpack(p_ref, w_ref, mu_ref):
    row, lane = iota((HALF, HD), 0), iota((HALF, HD), 1)
    means = []
    for h in range(GROUP):
        o, i = divmod(h, HP)
        packed = p_ref[o, i * PACK : i * PACK + HALF, :]
        tail = p_ref[o, i * PACK + HALF : (i + 1) * PACK, :]
        diag = tail[1:2]
        means.append(tail[0:1])
        top = jnp.where(row < lane, 2.0 * packed, jnp.where(row == lane, diag, 0.0))
        turned = pltpu.roll(packed, HALF, 1)
        down = lane - HALF
        low = jnp.where(down < row, 2.0 * turned, jnp.where(down == row, diag, 0.0))
        low = jnp.where(down >= 0, low, 0.0)
        w_ref[h * HD : h * HD + HALF, :] = top.astype(BF16)
        w_ref[h * HD + HALF : (h + 1) * HD, :] = low.astype(BF16)
    mean = jnp.concatenate(means, axis=0)
    m1 = mean.astype(BF16)
    rest = mean - m1.astype(F32)
    m2 = rest.astype(BF16)
    m3 = (rest - m2.astype(F32)).astype(BF16)
    mu_ref[0:GROUP, :] = m1
    mu_ref[GROUP : 2 * GROUP, :] = m2
    mu_ref[2 * GROUP :, :] = m3


def logits_kernel(copies, sc_ref, p_ref, kt_ref, prev_ref, w_out, st_out, w_ref, mu_ref, kf_ref, lg_ref):
    g, t = pl.program_id(0), pl.program_id(1)
    tile = kt_ref.shape[1]
    step = 256

    @pl.when(t == 0)
    def _():
        unpack(p_ref, w_ref, mu_ref)

    kf_ref[...] = kt_ref[...].astype(F32)
    rows = pl.ds(pl.multiple_of(g * GROUP, GROUP), GROUP)
    for s in range(0, tile, step):
        kt = kt_ref[:, s : s + step]
        kf = kf_ref[:, s : s + step]
        lin = jnp.dot(mu_ref[...], kt, preferred_element_type=F32)
        lin = (lin[:GROUP] + lin[GROUP : 2 * GROUP]) + lin[2 * GROUP :]
        quad = []
        for h in range(GROUP):
            m = jnp.dot(w_ref[h * HD : (h + 1) * HD, :], kt, preferred_element_type=F32)
            quad.append(jnp.sum(m * kf, axis=0, keepdims=True))
        quad = jnp.concatenate(quad, axis=0)
        cols = pl.ds(pl.multiple_of(t * tile + s, step), step)
        lg_ref[rows, cols] = quad * (0.5 / HD) + lin * (1.0 / math.sqrt(HD))

    @pl.when((g == pl.num_programs(0) - 1) & (t == pl.num_programs(1) - 1))
    def _():
        heads, width = lg_ref.shape
        lg = lg_ref[...]
        live = sc_ref[1] + iota((heads, width), 1) < sc_ref[2]
        peak = jnp.max(jnp.where(live, lg, -1e30), axis=1, keepdims=True)
        w = jnp.where(live, jnp.exp(jnp.where(live, lg - peak, 0.0)), 0.0)
        w_out[...] = w
        total = jnp.sum(w, axis=1, keepdims=True)
        at = sc_ref[0] * GROUP + iota((heads, 2 * H), 0)
        lane = iota((heads, 2 * H), 1)
        both = jnp.where(lane == at, peak, 0.0) + jnp.where(lane == at + H, total, 0.0)
        st = jnp.sum(both, axis=0, keepdims=True) + prev_ref[0:1, :]
        st_out[...] = jnp.broadcast_to(st, (copies, 2 * H))


def scores_kernel(sc_ref, all_ref, mine_ref, wa_ref, wb_ref, vn_ref, out_ref, ca_ref, cb_ref):
    @pl.when(pl.program_id(0) == 0)
    def _():
        every = all_ref[...]
        lane = iota((1, 2 * H), 1)
        peaks = every
        peak = jnp.max(peaks, axis=0, keepdims=True)
        sums = pltpu.roll(every, H, 1)
        valid = iota(every.shape, 1) < H
        total = jnp.sum(jnp.where(valid, jnp.exp(jnp.where(valid, peaks - peak, 0.0)) * sums, 0.0), axis=0, keepdims=True)
        ok = lane < H
        mine = mine_ref[0:1, :]
        scale = jnp.where(ok, jnp.exp(jnp.where(ok, mine - peak, 0.0)) / jnp.where(ok, total, 1.0), 0.0)
        shape = (OWN_HEADS, 2 * H)
        for ref, first in ((ca_ref, sc_ref[0] * GROUP), (cb_ref, (OWN_GROUPS - sc_ref[0]) * GROUP)):
            pick = iota(shape, 1) == first + iota(shape, 0)
            ref[...] = jnp.broadcast_to(jnp.sum(jnp.where(pick, scale, 0.0), axis=1, keepdims=True), ref.shape)

    width = out_ref.shape[1]

    def sums_of(w_ref, c_ref):
        w = w_ref[...] * c_ref[:, 0:1]
        return jnp.sum(w.reshape(OWN_GROUPS, GROUP, width), axis=1)

    a, b = sums_of(wa_ref, ca_ref), sums_of(wb_ref, cb_ref)
    first = sc_ref[0] == 0
    low, high = jnp.where(first, a, b), jnp.where(first, b, a)
    positions = sc_ref[3].astype(F32)
    out_ref[...] = jnp.concatenate([low, high], axis=0) * (positions / GROUP) * vn_ref[...]


def params(**kw):
    return pltpu.CompilerParams(vmem_limit_bytes=VMEM_LIMIT, **kw)


def local(queries, query_positions, keys, cache_values, cache_length):
    devices = NZ * NY * NC * NX
    n = keys.shape[0]
    nq = queries.shape[0]
    freqs = jnp.exp(-jnp.arange(HALF, dtype=F32) * (2.0 * math.log(1000000.0) / HD))
    angle = query_positions.astype(F32)[:, None] * freqs[None, :]
    cosine, sine = jnp.cos(angle), jnp.sin(angle)
    cosine = jnp.tile(jnp.concatenate([cosine, cosine], axis=1), (HP, 1))
    sine = jnp.tile(jnp.concatenate([-sine, sine], axis=1), (HP, 1))
    sent = pl.pallas_call(
        rotate_kernel,
        out_shape=jax.ShapeDtypeStruct((devices, HP * nq, HD), F32),
        compiler_params=params(),
        name="rotate",
    )(queries, cosine, sine)
    rotated = lax.all_to_all(sent, AXES, 0, 0)

    block = 512
    kt, vnorm = pl.pallas_call(
        prep_kernel,
        grid=(n // block,),
        in_specs=[pl.BlockSpec((block, KVH * HD), lambda i: (i, 0))] * 2,
        out_specs=[pl.BlockSpec((KVH * HD, block), lambda i: (0, i)), pl.BlockSpec((KVH, block), lambda i: (0, i))],
        out_shape=[jax.ShapeDtypeStruct((KVH * HD, n), BF16), jax.ShapeDtypeStruct((KVH, n), F32)],
        compiler_params=params(),
        cost_estimate=pl.CostEstimate(flops=2 * n * 512 * 32, bytes_accessed=12 * 2**20, transcendentals=0),
        name="prep",
    )(keys, cache_values)

    packed = pl.pallas_call(
        stats_kernel,
        out_shape=jax.ShapeDtypeStruct((OWNERS, HP * PACK, HD), F32),
        compiler_params=params(),
        name="stats",
    )(rotated)
    mine = lax.all_to_all(packed, ("z", "y"), 0, 0)
    other = lax.ppermute(mine, "c", [(0, 1), (1, 0)])

    core = lax.axis_index("c")
    start = lax.axis_index(AXES) * n
    everywhere = n * devices

    def scalars(which):
        return jnp.stack([which * OWN_GROUPS, start, cache_length[0], jnp.int32(everywhere)]).astype(jnp.int32)

    tile = 2048
    groups = OWNERS * HP // GROUP
    owners = OWNERS // groups

    def logits(which, stats, prev, copies, name):
        return pl.pallas_call(
            lambda *refs: logits_kernel(copies, *refs),
            grid_spec=pltpu.PrefetchScalarGridSpec(
                num_scalar_prefetch=1,
                grid=(groups, n // tile),
                in_specs=[
                    pl.BlockSpec((owners, HP * PACK, HD), lambda g, t, sc: (g, 0, 0)),
                    pl.BlockSpec((HD, tile), lambda g, t, sc: (sc[0] + g, t)),
                    pl.BlockSpec((8, 2 * H), lambda g, t, sc: (0, 0)),
                ],
                out_specs=[
                    pl.BlockSpec((OWN_HEADS, n), lambda g, t, sc: (0, 0)),
                    pl.BlockSpec((copies, 2 * H), lambda g, t, sc: (0, 0)),
                ],
                scratch_shapes=[
                    pltpu.VMEM((GROUP * HD, HD), BF16),
                    pltpu.VMEM((3 * GROUP, HD), BF16),
                    pltpu.VMEM((HD, tile), F32),
                    pltpu.VMEM((OWN_HEADS, n), F32),
                ],
            ),
            out_shape=[
                jax.ShapeDtypeStruct((OWN_HEADS, n), F32),
                jax.ShapeDtypeStruct((copies, 2 * H), F32),
            ],
            compiler_params=params(),
            cost_estimate=pl.CostEstimate(
                flops=2 * n * OWN_HEADS * HD * HD, bytes_accessed=4 * 2**20, transcendentals=n * OWN_HEADS
            ),
            name=name,
        )(scalars(which), stats, kt, prev)

    w_mine, st_mine = logits(core, mine, jnp.zeros((8, 2 * H), F32), 8, "logits_own")
    w_other, st = logits(1 - core, other, st_mine, devices, "logits_other")
    every = lax.all_to_all(st, AXES, 0, 0)

    part = n // 2
    return pl.pallas_call(
        scores_kernel,
        grid_spec=pltpu.PrefetchScalarGridSpec(
            num_scalar_prefetch=1,
            grid=(n // part,),
            in_specs=[
                pl.BlockSpec((devices, 2 * H), lambda i, sc: (0, 0)),
                pl.BlockSpec((8, 2 * H), lambda i, sc: (0, 0)),
                pl.BlockSpec((OWN_HEADS, part), lambda i, sc: (0, i)),
                pl.BlockSpec((OWN_HEADS, part), lambda i, sc: (0, i)),
                pl.BlockSpec((KVH, part), lambda i, sc: (0, i)),
            ],
            out_specs=pl.BlockSpec((KVH, part), lambda i, sc: (0, i)),
            scratch_shapes=[pltpu.VMEM((OWN_HEADS, HD), F32)] * 2,
        ),
        out_shape=jax.ShapeDtypeStruct((KVH, n), F32),
        compiler_params=params(),
        name="scores",
    )(scalars(core), every, st, w_mine, w_other, vnorm)


def solution(mesh):
    fine = Mesh(mesh.devices.reshape(NZ, NY, NC, NX), AXES)
    return jax.shard_map(
        local,
        mesh=fine,
        in_specs=(P(AXES, None), P(AXES), P(AXES, None), P(AXES, None), P()),
        out_specs=P(None, AXES),
        check_vma=False,
    )
```

```python
import functools
import math

import jax
import jax.numpy as jnp
from jax import lax
from jax.experimental import pallas as pl
from jax.experimental.pallas import tpu as pltpu
from jax.sharding import Mesh
from jax.sharding import PartitionSpec as P

H = 64
KVH = 4
HD = 128
QN = 512
GROUP = H // KVH
HALF = HD // 2
AXES = ("z", "y", "c", "x")
NZ, NY, NC, NX = 4, 4, 2, 4
DEVICES = NZ * NY * NC * NX
OWNERS = NZ * NY
PLANES = OWNERS * NC
HP = H // PLANES
PACK = HP * HALF + 8
OWN_HEADS = H // NC
OWN_GROUPS = KVH // NC
GROUP_OWNERS = OWNERS // OWN_GROUPS
F32 = jnp.float32
BF16 = jnp.bfloat16
VMEM = pl.BlockSpec(memory_space=pltpu.VMEM)
SMEM = pl.BlockSpec(memory_space=pltpu.SMEM)
HBM = pl.BlockSpec(memory_space=pltpu.HBM)


def iota(shape, dim):
    return lax.broadcasted_iota(jnp.int32, shape, dim)


def rotate_kernel(pos_hbm, q_hbm, out_ref, pos_ref, q_ref, sems):
    nq = q_ref.shape[0]
    pos_copy = pltpu.make_async_copy(pos_hbm, pos_ref, sems.at[0])
    q_copy = pltpu.make_async_copy(q_hbm, q_ref, sems.at[1])
    pos_copy.start()
    q_copy.start()
    rows = HP * nq
    query = lax.rem(iota((rows, HD), 0), nq)
    lane = iota((rows, HD), 1)
    position = jnp.zeros((rows, HD), F32)
    pos_copy.wait()
    for i in range(nq):
        position = jnp.where(query == i, pos_ref[i].astype(F32), position)
    freqs = jnp.exp(-lax.rem(lane, HALF).astype(F32) * (2.0 * math.log(1000000.0) / HD))
    angle = position * freqs
    cos, sin = jnp.cos(angle), jnp.sin(angle)
    sin = jnp.where(lane < HALF, -sin, sin)
    q_copy.wait()
    for plane in range(PLANES):
        zy, core = divmod(plane, NC)
        head = core * OWN_HEADS + zy * HP
        v = jnp.concatenate(
            [q_ref[:, (head + i) * HD : (head + i + 1) * HD].astype(F32) for i in range(HP)], axis=0
        )
        r = v * cos + pltpu.roll(v, HALF, 1) * sin
        for x in range(NX):
            out_ref[plane * NX + x] = r


def stats_kernel(r_ref, out_ref):
    half = r_ref.shape[0] // 2
    rows = half * r_ref.shape[1]
    nq = r_ref.shape[1] // HP
    xa = r_ref[:half].reshape(rows, HD)
    xb = r_ref[half:].reshape(rows, HD)
    first = lax.rem(iota((rows, HD), 0), r_ref.shape[1]) < nq
    heads = (
        jnp.where(first, xa, pltpu.roll(xb, nq, 0)),
        jnp.where(first, pltpu.roll(xa, rows - nq, 0), xb),
    )
    row_h, lane_h = iota((HALF, HD), 0), iota((HALF, HD), 1)
    eye = iota((HD, HD), 0) == iota((HD, HD), 1)
    tail = []
    for i, x in enumerate(heads):
        second = lax.dot_general(
            x, x, (((0,), (0,)), ((), ())), precision=lax.Precision.HIGHEST, preferred_element_type=F32
        )
        mean = jnp.sum(x, axis=0, keepdims=True) * (1.0 / QN)
        mean_col = jnp.sum(jnp.where(eye, mean, 0.0), axis=1, keepdims=True)
        sigma = second * (1.0 / QN) - mean_col * mean
        diag = jnp.sum(jnp.where(eye, sigma, 0.0), axis=0, keepdims=True)
        packed = jnp.where(row_h < lane_h, sigma[:HALF], pltpu.roll(sigma[HALF:], HALF, 1))
        for o in range(OWNERS):
            out_ref[o, i * HALF : (i + 1) * HALF, :] = packed
        tail += [mean, diag]
    tail = jnp.concatenate(tail + [jnp.zeros((8 - 2 * HP, HD), F32)], axis=0)
    for o in range(OWNERS):
        out_ref[o, HP * HALF :, :] = tail


def prep_kernel(k_ref, v_ref, own_ref, other_ref, vn_ref):
    wide = OWN_GROUPS * HD
    low, high = k_ref[:, :wide], k_ref[:, wide:]
    first = lax.axis_index("c") == 0
    own_ref[...] = jnp.where(first, low, high).T
    other_ref[...] = jnp.where(first, high, low).T
    ones = jnp.ones((8, HD), BF16)
    nt = (((1,), (1,)), ((), ()))
    for g in range(KVH):
        v = v_ref[:, g * HD : (g + 1) * HD].astype(F32)
        sq = v * v
        hi = sq.astype(BF16)
        lo = (sq - hi.astype(F32)).astype(BF16)
        s = lax.dot_general(ones, hi, nt, preferred_element_type=F32)
        s = s + lax.dot_general(ones, lo, nt, preferred_element_type=F32)
        vn_ref[g : g + 1, :] = jnp.sqrt(s[:1] * (1.0 / HD))


def unpack(p_ref, g, w_ref, mu_ref):
    row, lane = iota((HALF, HD), 0), iota((HALF, HD), 1)
    down = lane - HALF
    means = []
    for h in range(GROUP):
        o, i = divmod(h, HP)
        packed = p_ref[g * GROUP_OWNERS + o, i * HALF : (i + 1) * HALF, :]
        tail = p_ref[g * GROUP_OWNERS + o, HP * HALF :, :]
        diag = tail[2 * i + 1 : 2 * i + 2]
        means.append(tail[2 * i : 2 * i + 1])
        top = jnp.where(row < lane, 2.0 * packed, jnp.where(row == lane, diag, 0.0))
        low = jnp.where(down < row, 2.0 * pltpu.roll(packed, HALF, 1), jnp.where(down == row, diag, 0.0))
        low = jnp.where(down >= 0, low, 0.0)
        w_ref[h * HD : h * HD + HALF, :] = top.astype(BF16)
        w_ref[h * HD + HALF : (h + 1) * HD, :] = low.astype(BF16)
    mean = jnp.concatenate(means, axis=0)
    m1 = mean.astype(BF16)
    rest = mean - m1.astype(F32)
    m2 = rest.astype(BF16)
    m3 = (rest - m2.astype(F32)).astype(BF16)
    mu_ref[0:GROUP, :] = m1
    mu_ref[GROUP : 2 * GROUP, :] = m2
    mu_ref[2 * GROUP :, :] = m3


def logits_kernel(own, len_ref, p_ref, kt_ref, *refs):
    prev_ref, (w_out, st_out, w_ref, mu_ref) = (None, refs) if own else (refs[0], refs[1:])
    core = lax.axis_index("c")
    side = core if own else 1 - core
    width = kt_ref.shape[1]
    step = 256

    def group(g, carry):
        unpack(p_ref, g, w_ref, mu_ref)
        base = pl.multiple_of(g * HD, HD)
        rows = pl.ds(pl.multiple_of(g * GROUP, GROUP), GROUP)
        for s in range(0, width, step):
            kt = kt_ref[pl.ds(base, HD), s : s + step]
            kf = kt.astype(F32)
            lin = jnp.dot(mu_ref[...], kt, preferred_element_type=F32)
            lin = (lin[:GROUP] + lin[GROUP : 2 * GROUP]) + lin[2 * GROUP :]
            quad = []
            for h in range(GROUP):
                m = jnp.dot(w_ref[h * HD : (h + 1) * HD, :], kt, preferred_element_type=F32)
                quad.append(jnp.sum(m * kf, axis=0, keepdims=True))
            quad = jnp.concatenate(quad, axis=0)
            w_out[rows, s : s + step] = quad * (0.5 / HD) + lin * (1.0 / math.sqrt(HD))
        return carry

    lax.fori_loop(0, OWN_GROUPS, group, 0)
    lg = w_out[...]
    live = lax.axis_index(AXES) * width + iota(lg.shape, 1) < len_ref[0]
    peak = jnp.max(jnp.where(live, lg, -1e30), axis=1, keepdims=True)
    w = jnp.where(live, jnp.exp(jnp.where(live, lg - peak, 0.0)), 0.0)
    w_out[...] = w
    total = jnp.sum(w, axis=1, keepdims=True)
    shape = (OWN_HEADS, 2 * H)
    lane, at = iota(shape, 1), side * OWN_HEADS + iota(shape, 0)
    both = jnp.where(lane == at, peak, 0.0) + jnp.where(lane == at + H, total, 0.0)
    st = jnp.sum(both, axis=0, keepdims=True)
    if not own:
        st = st + prev_ref[0:1, :]
    st_out[...] = jnp.broadcast_to(st, st_out.shape)


def scores_kernel(all_ref, mine_ref, wa_ref, wb_ref, vn_ref, out_ref):
    core = lax.axis_index("c")
    every = all_ref[...]
    valid = iota(every.shape, 1) < H
    peak = jnp.max(every, axis=0, keepdims=True)
    sums = pltpu.roll(every, H, 1)
    total = jnp.where(valid, jnp.exp(jnp.where(valid, every - peak, 0.0)) * sums, 0.0)
    total = jnp.sum(total, axis=0, keepdims=True)
    ok = valid[:1]
    mine = jnp.exp(jnp.where(ok, mine_ref[0:1, :] - peak, 0.0))
    scale = jnp.where(ok, mine / jnp.where(ok, total, 1.0), 0.0)
    shape = (OWN_HEADS, 2 * H)
    width = out_ref.shape[1]

    def sums_of(w_ref, side):
        pick = iota(shape, 1) == side * OWN_HEADS + iota(shape, 0)
        column = jnp.sum(jnp.where(pick, scale, 0.0), axis=1, keepdims=True)
        return jnp.sum((w_ref[...] * column).reshape(OWN_GROUPS, GROUP, width), axis=1)

    a, b = sums_of(wa_ref, core), sums_of(wb_ref, 1 - core)
    low, high = jnp.where(core == 0, a, b), jnp.where(core == 0, b, a)
    out_ref[...] = jnp.concatenate([low, high], axis=0) * (width * DEVICES / GROUP) * vn_ref[...]


def params(mib):
    return pltpu.CompilerParams(vmem_limit_bytes=mib * 2**20)


def local(queries, query_positions, keys, cache_values, cache_length):
    n = keys.shape[0]
    nq = queries.shape[0]
    sent = pl.pallas_call(
        rotate_kernel,
        in_specs=[HBM, HBM],
        out_specs=VMEM,
        out_shape=jax.ShapeDtypeStruct((DEVICES, HP * nq, HD), F32),
        scratch_shapes=[
            pltpu.SMEM((nq,), jnp.int32),
            pltpu.VMEM(queries.shape, BF16),
            pltpu.SemaphoreType.DMA((2,)),
        ],
        compiler_params=params(58),
        name="rotate",
    )(query_positions, queries)
    rotated = lax.all_to_all(sent, AXES, 0, 0)

    block = 1024
    half = pl.BlockSpec((OWN_GROUPS * HD, block), lambda i: (0, i))
    half_shape = jax.ShapeDtypeStruct((OWN_GROUPS * HD, n), BF16)
    kt_own, kt_other, vnorm = pl.pallas_call(
        prep_kernel,
        grid=(n // block,),
        in_specs=[pl.BlockSpec((block, KVH * HD), lambda i: (i, 0))] * 2,
        out_specs=[half, half, pl.BlockSpec((KVH, block), lambda i: (0, i))],
        out_shape=[half_shape, half_shape, jax.ShapeDtypeStruct((KVH, n), F32)],
        compiler_params=params(56),
        cost_estimate=pl.CostEstimate(flops=2 * n * 512 * 512, bytes_accessed=12 * 2**20, transcendentals=0),
        name="prep",
    )(keys, cache_values)
    rotated, kt_own, kt_other, vnorm = lax.optimization_barrier((rotated, kt_own, kt_other, vnorm))

    packed = pl.pallas_call(
        stats_kernel,
        in_specs=[VMEM],
        out_specs=VMEM,
        out_shape=jax.ShapeDtypeStruct((OWNERS, PACK, HD), F32),
        compiler_params=params(16),
        name="stats",
    )(rotated)
    mine = lax.all_to_all(packed, ("z", "y"), 0, 0)
    other = lax.ppermute(mine, "c", [(0, 1), (1, 0)])

    def logits(stats, kt, prev, copies):
        own = prev is None
        return pl.pallas_call(
            functools.partial(logits_kernel, own),
            in_specs=[SMEM, VMEM, VMEM] + [VMEM] * (not own),
            out_specs=[VMEM, VMEM],
            out_shape=[
                jax.ShapeDtypeStruct((OWN_HEADS, n), F32),
                jax.ShapeDtypeStruct((copies, 2 * H), F32),
            ],
            scratch_shapes=[pltpu.VMEM((GROUP * HD, HD), BF16), pltpu.VMEM((3 * GROUP, HD), BF16)],
            compiler_params=params(16),
            cost_estimate=pl.CostEstimate(
                flops=2 * n * OWN_HEADS * HD * HD, bytes_accessed=4 * 2**20, transcendentals=n * OWN_HEADS
            ),
            name="logits_own" if own else "logits_other",
        )(cache_length, stats, kt, *(() if own else (prev,)))

    w_mine, st_mine = logits(mine, kt_own, None, 8)
    w_other, st = logits(other, kt_other, st_mine, DEVICES)
    every = lax.all_to_all(st, AXES, 0, 0)

    return pl.pallas_call(
        scores_kernel,
        in_specs=[VMEM] * 5,
        out_specs=VMEM,
        out_shape=jax.ShapeDtypeStruct((KVH, n), F32),
        compiler_params=params(16),
        name="scores",
    )(every, st, w_mine, w_other, vnorm)


def solution(mesh):
    fine = Mesh(mesh.devices.reshape(NZ, NY, NC, NX), AXES)
    return jax.shard_map(
        local,
        mesh=fine,
        in_specs=(P(AXES, None), P(AXES), P(AXES, None), P(AXES, None), P()),
        out_specs=P(None, AXES),
        check_vma=False,
    )
```

```python
import functools
import math

import jax
import jax.numpy as jnp
from jax import lax
from jax.experimental import pallas as pl
from jax.experimental.pallas import tpu as pltpu
from jax.sharding import Mesh
from jax.sharding import PartitionSpec as P

H = 64
KVH = 4
HD = 128
QN = 512
GROUP = H // KVH
HALF = HD // 2
AXES = ("z", "y", "c", "x")
NZ, NY, NC, NX = 4, 4, 2, 4
DEVICES = NZ * NY * NC * NX
OWNERS = NZ * NY
PLANES = OWNERS * NC
CHUNKS = H // PLANES
PACK = HALF + 8
OWN_HEADS = H // NC
PARTS = ((0, 0), (0, 1), (1, 0), (1, 1))
F32 = jnp.float32
BF16 = jnp.bfloat16
VMEM = pl.BlockSpec(memory_space=pltpu.VMEM)
SMEM = pl.BlockSpec(memory_space=pltpu.SMEM)
HBM = pl.BlockSpec(memory_space=pltpu.HBM)


def iota(shape, dim):
    return lax.broadcasted_iota(jnp.int32, shape, dim)


def rotate_kernel(pos_hbm, q_hbm, out_ref, pos_ref, q_ref, sems):
    nq = q_ref.shape[0]
    pos_copy = pltpu.make_async_copy(pos_hbm, pos_ref, sems.at[0])
    q_copy = pltpu.make_async_copy(q_hbm, q_ref, sems.at[1])
    pos_copy.start()
    q_copy.start()
    query, lane = iota((nq, HD), 0), iota((nq, HD), 1)
    position = jnp.zeros((nq, HD), F32)
    pos_copy.wait()
    for i in range(nq):
        position = jnp.where(query == i, pos_ref[i].astype(F32), position)
    freqs = jnp.exp(-lax.rem(lane, HALF).astype(F32) * (2.0 * math.log(1000000.0) / HD))
    angle = position * freqs
    cos, sin = jnp.cos(angle), jnp.sin(angle)
    sin = jnp.where(lane < HALF, -sin, sin)
    q_copy.wait()
    for chunk in range(CHUNKS):
        for plane in range(PLANES):
            zy, core = divmod(plane, NC)
            head = core * OWN_HEADS + chunk * GROUP + zy
            v = q_ref[:, head * HD : (head + 1) * HD].astype(F32)
            r = v * cos + pltpu.roll(v, HALF, 1) * sin
            for x in range(chunk, NX, CHUNKS):
                out_ref[plane * NX + x] = r


def stats_kernel(r_ref, out_ref):
    half = r_ref.shape[0] // 2
    x = jnp.concatenate([r_ref[:half], r_ref[half:]], axis=1).reshape(QN, HD)
    row_h, lane_h = iota((HALF, HD), 0), iota((HALF, HD), 1)
    eye = iota((HD, HD), 0) == iota((HD, HD), 1)
    second = lax.dot_general(
        x, x, (((0,), (0,)), ((), ())), precision=lax.Precision.HIGHEST, preferred_element_type=F32
    )
    mean = jnp.sum(x, axis=0, keepdims=True) * (1.0 / QN)
    mean_col = jnp.sum(jnp.where(eye, mean, 0.0), axis=1, keepdims=True)
    sigma = second * (1.0 / QN) - mean_col * mean
    diag = jnp.sum(jnp.where(eye, sigma, 0.0), axis=0, keepdims=True)
    packed = jnp.where(row_h < lane_h, sigma[:HALF], pltpu.roll(sigma[HALF:], HALF, 1))
    tail = jnp.concatenate([mean, diag, jnp.zeros((PACK - HALF - 2, HD), F32)], axis=0)
    for o in range(OWNERS):
        out_ref[o, :HALF, :] = packed
        out_ref[o, HALF:, :] = tail


def place(far, other):
    chunk, side = lax.rem(lax.axis_index("x"), CHUNKS), lax.axis_index("c")
    return (1 - chunk if far else chunk), (1 - side if other else side)


def prep_kernel(k_ref, v_ref, *refs):
    kt_refs, vn_ref = refs[:-1], refs[-1]
    for part, kt_ref in zip(PARTS, kt_refs):
        chunk, side = place(*part)
        low, high = k_ref[:, : CHUNKS * HD], k_ref[:, CHUNKS * HD :]
        k = jnp.where(side == 0, low, high)
        kt_ref[...] = jnp.where(chunk == 0, k[:, :HD], k[:, HD:]).T
    ones = jnp.ones((8, HD), BF16)
    nt = (((1,), (1,)), ((), ()))
    for g in range(KVH):
        v = v_ref[:, g * HD : (g + 1) * HD].astype(F32)
        sq = v * v
        hi = sq.astype(BF16)
        lo = (sq - hi.astype(F32)).astype(BF16)
        s = lax.dot_general(ones, hi, nt, preferred_element_type=F32)
        s = s + lax.dot_general(ones, lo, nt, preferred_element_type=F32)
        vn_ref[g : g + 1, :] = jnp.sqrt(s[:1] * (1.0 / HD))


def unpack(p_ref, w_ref, mu_ref):
    row, lane = iota((HALF, HD), 0), iota((HALF, HD), 1)
    down = lane - HALF
    means = []
    for h in range(GROUP):
        packed, tail = p_ref[h, :HALF, :], p_ref[h, HALF:, :]
        means.append(tail[0:1])
        diag = tail[1:2]
        top = jnp.where(row < lane, 2.0 * packed, jnp.where(row == lane, diag, 0.0))
        low = jnp.where(down < row, 2.0 * pltpu.roll(packed, HALF, 1), jnp.where(down == row, diag, 0.0))
        low = jnp.where(down >= 0, low, 0.0)
        w_ref[h * HD : h * HD + HALF, :] = top.astype(BF16)
        w_ref[h * HD + HALF : (h + 1) * HD, :] = low.astype(BF16)
    mean = jnp.concatenate(means, axis=0)
    m1 = mean.astype(BF16)
    rest = mean - m1.astype(F32)
    m2 = rest.astype(BF16)
    m3 = (rest - m2.astype(F32)).astype(BF16)
    mu_ref[0:GROUP, :] = m1
    mu_ref[GROUP : 2 * GROUP, :] = m2
    mu_ref[2 * GROUP :, :] = m3


def logits_kernel(part, len_ref, p_ref, kt_ref, *refs):
    w_out, st_out, w_ref, mu_ref = refs[-4:]
    chunk, side = place(*part)
    width = kt_ref.shape[1]
    step = 256
    unpack(p_ref, w_ref, mu_ref)
    for s in range(0, width, step):
        kt = kt_ref[:, s : s + step]
        kf = kt.astype(F32)
        lin = jnp.dot(mu_ref[...], kt, preferred_element_type=F32)
        lin = (lin[:GROUP] + lin[GROUP : 2 * GROUP]) + lin[2 * GROUP :]
        quad = []
        for h in range(GROUP):
            m = jnp.dot(w_ref[h * HD : (h + 1) * HD, :], kt, preferred_element_type=F32)
            quad.append(jnp.sum(m * kf, axis=0, keepdims=True))
        quad = jnp.concatenate(quad, axis=0)
        w_out[:, s : s + step] = quad * (0.5 / HD) + lin * (1.0 / math.sqrt(HD))
    lg = w_out[...]
    live = lax.axis_index(AXES) * width + iota(lg.shape, 1) < len_ref[0]
    peak = jnp.max(jnp.where(live, lg, -1e30), axis=1, keepdims=True)
    w = jnp.where(live, jnp.exp(jnp.where(live, lg - peak, 0.0)), 0.0)
    w_out[...] = w
    total = jnp.sum(w, axis=1, keepdims=True)
    shape = (GROUP, 2 * H)
    lane, at = iota(shape, 1), side * OWN_HEADS + chunk * GROUP + iota(shape, 0)
    both = jnp.where(lane == at, peak, 0.0) + jnp.where(lane == at + H, total, 0.0)
    st = jnp.sum(both, axis=0, keepdims=True)
    if len(refs) > 4:
        st = st + refs[0][0:1, :]
    st_out[...] = jnp.broadcast_to(st, st_out.shape)


def scores_kernel(all_ref, mine_ref, *refs):
    w_refs, vn_ref, out_ref = refs[:-2], refs[-2], refs[-1]
    every = all_ref[...]
    valid = iota(every.shape, 1) < H
    peak = jnp.max(every, axis=0, keepdims=True)
    sums = pltpu.roll(every, H, 1)
    total = jnp.where(valid, jnp.exp(jnp.where(valid, every - peak, 0.0)) * sums, 0.0)
    total = jnp.sum(total, axis=0, keepdims=True)
    ok = valid[:1]
    mine = jnp.exp(jnp.where(ok, mine_ref[0:1, :] - peak, 0.0))
    scale = jnp.where(ok, mine / jnp.where(ok, total, 1.0), 0.0)
    shape = (GROUP, 2 * H)
    width = out_ref.shape[1]

    def sums_of(w_ref, part):
        chunk, side = place(*part)
        pick = iota(shape, 1) == side * OWN_HEADS + chunk * GROUP + iota(shape, 0)
        column = jnp.sum(jnp.where(pick, scale, 0.0), axis=1, keepdims=True)
        return side * CHUNKS + chunk, jnp.sum(w_ref[...] * column, axis=0, keepdims=True)

    group = iota(out_ref.shape, 0)
    out = jnp.zeros(out_ref.shape, F32)
    for part, w_ref in zip(PARTS, w_refs):
        which, row = sums_of(w_ref, part)
        out = jnp.where(group == which, row, out)
    out_ref[...] = out * (width * DEVICES / GROUP) * vn_ref[...]


def params(mib):
    return pltpu.CompilerParams(vmem_limit_bytes=mib * 2**20)


def local(queries, query_positions, keys, cache_values, cache_length):
    n = keys.shape[0]
    nq = queries.shape[0]
    sent = pl.pallas_call(
        rotate_kernel,
        in_specs=[HBM, HBM],
        out_specs=VMEM,
        out_shape=jax.ShapeDtypeStruct((DEVICES, nq, HD), F32),
        scratch_shapes=[
            pltpu.SMEM((nq,), jnp.int32),
            pltpu.VMEM(queries.shape, BF16),
            pltpu.SemaphoreType.DMA((2,)),
        ],
        compiler_params=params(58),
        name="rotate",
    )(query_positions, queries)
    rotated = lax.all_to_all(sent, AXES, 0, 0)

    block = 1024
    turned = pl.BlockSpec((HD, block), lambda i: (0, i))
    *keys_t, vnorm = pl.pallas_call(
        prep_kernel,
        grid=(n // block,),
        in_specs=[pl.BlockSpec((block, KVH * HD), lambda i: (i, 0))] * 2,
        out_specs=[turned] * KVH + [pl.BlockSpec((KVH, block), lambda i: (0, i))],
        out_shape=[jax.ShapeDtypeStruct((HD, n), BF16)] * KVH + [jax.ShapeDtypeStruct((KVH, n), F32)],
        compiler_params=params(51),
        cost_estimate=pl.CostEstimate(flops=2 * n * 512 * 512, bytes_accessed=12 * 2**20, transcendentals=0),
        name="prep",
    )(keys, cache_values)
    rotated, keys_t, vnorm = lax.optimization_barrier((rotated, keys_t, vnorm))

    packed = pl.pallas_call(
        stats_kernel,
        in_specs=[VMEM],
        out_specs=VMEM,
        out_shape=jax.ShapeDtypeStruct((OWNERS, PACK, HD), F32),
        compiler_params=params(16),
        name="stats",
    )(rotated)
    swap = [(0, 1), (1, 0)]
    ring = [(x, (x + 1) % NX) for x in range(NX)] + [(NX + x, NX + (x - 1) % NX) for x in range(NX)]
    mine = lax.all_to_all(packed, ("z", "y"), 0, 0)
    far = lax.ppermute(mine, ("c", "x"), ring)
    stats = [mine, lax.ppermute(mine, "c", swap)]

    weights, st = [], ()
    for i, part in enumerate(PARTS):
        w, now = pl.pallas_call(
            functools.partial(logits_kernel, part),
            in_specs=[SMEM] + [VMEM] * (2 + len(st)),
            out_specs=[VMEM, VMEM],
            out_shape=[
                jax.ShapeDtypeStruct((GROUP, n), F32),
                jax.ShapeDtypeStruct((DEVICES if i == KVH - 1 else 8, 2 * H), F32),
            ],
            scratch_shapes=[pltpu.VMEM((GROUP * HD, HD), BF16), pltpu.VMEM((3 * GROUP, HD), BF16)],
            compiler_params=params(16),
            cost_estimate=pl.CostEstimate(
                flops=2 * n * GROUP * HD * HD, bytes_accessed=2 * 2**20, transcendentals=n * GROUP
            ),
            name="logits",
        )(cache_length, stats[i], keys_t[i], *st)
        weights.append(w)
        if i == NC - 1:
            far, now = lax.optimization_barrier((far, now))
            stats += [far, lax.ppermute(far, "c", swap)]
        st = (now,)
    every = lax.all_to_all(st[0], AXES, 0, 0)

    return pl.pallas_call(
        scores_kernel,
        in_specs=[VMEM] * (3 + KVH),
        out_specs=VMEM,
        out_shape=jax.ShapeDtypeStruct((KVH, n), F32),
        compiler_params=params(16),
        name="scores",
    )(every, st[0], *weights, vnorm)


def solution(mesh):
    fine = Mesh(mesh.devices.reshape(NZ, NY, NC, NX), AXES)
    return jax.shard_map(
        local,
        mesh=fine,
        in_specs=(P(AXES, None), P(AXES), P(AXES, None), P(AXES, None), P()),
        out_specs=P(None, AXES),
        check_vma=False,
    )
```

```python
import functools
import math

import jax
import jax.numpy as jnp
from jax import lax
from jax.experimental import pallas as pl
from jax.experimental.pallas import tpu as pltpu
from jax.sharding import Mesh
from jax.sharding import PartitionSpec as P

H = 64
KVH = 4
HD = 128
QN = 512
GROUP = H // KVH
HALF = HD // 2
AXES = ("z", "y", "c", "x")
NZ, NY, NC, NX = 4, 4, 2, 4
DEVICES = NZ * NY * NC * NX
OWNERS = NZ * NY
PLANES = OWNERS * NC
CHUNKS = H // PLANES
PACK = HALF + 8
OWN_HEADS = H // NC
LAST = 8
ROWS = HD - LAST
PARTS = ((0, 0), (0, 1), (1, 0), (1, 1))
F32 = jnp.float32
BF16 = jnp.bfloat16
VMEM = pl.BlockSpec(memory_space=pltpu.VMEM)
SMEM = pl.BlockSpec(memory_space=pltpu.SMEM)
HBM = pl.BlockSpec(memory_space=pltpu.HBM)


def iota(shape, dim):
    return lax.broadcasted_iota(jnp.int32, shape, dim)


def rotate_kernel(pos_hbm, q_hbm, out_ref, pos_ref, q_ref, sems):
    nq = q_ref.shape[0]
    pos_copy = pltpu.make_async_copy(pos_hbm, pos_ref, sems.at[0])
    q_copy = pltpu.make_async_copy(q_hbm, q_ref, sems.at[1])
    pos_copy.start()
    q_copy.start()
    query, lane = iota((nq, HD), 0), iota((nq, HD), 1)
    position = jnp.zeros((nq, HD), F32)
    pos_copy.wait()
    for i in range(nq):
        position = jnp.where(query == i, pos_ref[i].astype(F32), position)
    freqs = jnp.exp(-lax.rem(lane, HALF).astype(F32) * (2.0 * math.log(1000000.0) / HD))
    angle = position * freqs
    cos, sin = jnp.cos(angle), jnp.sin(angle)
    sin = jnp.where(lane < HALF, -sin, sin)
    q_copy.wait()
    for chunk in range(CHUNKS):
        for plane in range(PLANES):
            zy, core = divmod(plane, NC)
            head = core * OWN_HEADS + chunk * GROUP + zy
            v = q_ref[:, head * HD : (head + 1) * HD].astype(F32)
            r = v * cos + pltpu.roll(v, HALF, 1) * sin
            for x in range(chunk, NX, CHUNKS):
                out_ref[plane * NX + x] = r


def stats_kernel(r_ref, out_ref):
    half = r_ref.shape[0] // 2
    x = jnp.concatenate([r_ref[:half], r_ref[half:]], axis=1).reshape(QN, HD)
    row_h, lane_h = iota((HALF, HD), 0), iota((HALF, HD), 1)
    eye = iota((HD, HD), 0) == iota((HD, HD), 1)
    second = lax.dot_general(
        x, x, (((0,), (0,)), ((), ())), precision=lax.Precision.HIGHEST, preferred_element_type=F32
    )
    mean = jnp.sum(x, axis=0, keepdims=True) * (1.0 / QN)
    mean_col = jnp.sum(jnp.where(eye, mean, 0.0), axis=1, keepdims=True)
    sigma = second * (1.0 / QN) - mean_col * mean
    diag = jnp.sum(jnp.where(eye, sigma, 0.0), axis=0, keepdims=True)
    packed = jnp.where(row_h < lane_h, sigma[:HALF], pltpu.roll(sigma[HALF:], HALF, 1))
    row_l, lane_l = iota((LAST, HD), 0), iota((LAST, HD), 1)
    corner = jnp.zeros((LAST, HD), F32)
    for i in range(LAST):
        moved = pltpu.roll(sigma[HALF : HALF + LAST], (LAST * i - HALF) % HD, 1)
        j = lane_l - LAST * i
        moved = jnp.where(j < i, 2.0 * moved, moved)
        corner = jnp.where((row_l == i) & (j >= 0) & (j <= i), moved, corner)
    corner = jnp.sum(corner, axis=0, keepdims=True)
    tail = jnp.concatenate([mean, diag, corner, jnp.zeros((PACK - HALF - 3, HD), F32)], axis=0)
    for o in range(OWNERS):
        out_ref[o, :HALF, :] = packed
        out_ref[o, HALF:, :] = tail


def place(far, other):
    chunk, side = lax.rem(lax.axis_index("x"), CHUNKS), lax.axis_index("c")
    return (1 - chunk if far else chunk), (1 - side if other else side)


def prep_kernel(len_ref, k_ref, v_ref, *refs):
    kt_refs, vn_ref, live_ref = refs[:-2], refs[-2], refs[-1]
    here = pl.num_programs(0) * k_ref.shape[0]
    live_ref[...] = jnp.full(live_ref.shape, len_ref[0] - lax.axis_index(AXES) * here, jnp.int32)
    for part, kt_ref in zip(PARTS, kt_refs):
        chunk, side = place(*part)
        low, high = k_ref[:, : CHUNKS * HD], k_ref[:, CHUNKS * HD :]
        k = jnp.where(side == 0, low, high)
        kt_ref[...] = jnp.where(chunk == 0, k[:, :HD], k[:, HD:]).T
    ones = jnp.ones((8, HD), BF16)
    nt = (((1,), (1,)), ((), ()))
    for g in range(KVH):
        v = v_ref[:, g * HD : (g + 1) * HD].astype(F32)
        sq = v * v
        hi = sq.astype(BF16)
        lo = (sq - hi.astype(F32)).astype(BF16)
        s = lax.dot_general(ones, hi, nt, preferred_element_type=F32)
        s = s + lax.dot_general(ones, lo, nt, preferred_element_type=F32)
        vn_ref[g : g + 1, :] = jnp.sqrt(s[:1] * (1.0 / HD))


def unpack(p_ref, w_ref, mu_ref, corner_ref):
    row, lane = iota((HALF, HD), 0), iota((HALF, HD), 1)
    down = lane - HALF
    means, corners, forms = [], [], []
    for h in range(GROUP):
        packed, tail = p_ref[h, :HALF, :], p_ref[h, HALF:, :]
        means.append(tail[0:1])
        diag = tail[1:2]
        corners.append(tail[2:3])
        top = jnp.where(row < lane, 2.0 * packed, jnp.where(row == lane, diag, 0.0))
        low = jnp.where(down < row, 2.0 * pltpu.roll(packed, HALF, 1), jnp.where(down == row, diag, 0.0))
        low = jnp.where(down >= 0, low, 0.0)
        forms += [top, low[LAST:]]
        if h % 2 == 1:
            w_ref[(h - 1) * ROWS : (h + 1) * ROWS, :] = jnp.concatenate(forms, axis=0).astype(BF16)
            forms = []
    mean = jnp.concatenate(means, axis=0)
    m1 = mean.astype(BF16)
    rest = mean - m1.astype(F32)
    m2 = rest.astype(BF16)
    m3 = (rest - m2.astype(F32)).astype(BF16)
    mu_ref[0:GROUP, :] = m1
    mu_ref[GROUP : 2 * GROUP, :] = m2
    mu_ref[2 * GROUP :, :] = m3
    corner = jnp.concatenate(corners, axis=0).astype(BF16).astype(F32)
    for i in range(LAST):
        for j in range(i + 1):
            at = LAST * i + j
            corner_ref[at] = jnp.broadcast_to(corner[:, at : at + 1], (GROUP, HD))


def corner_sum(corner_ref, kf):
    width = kf.shape[1]
    last = [jnp.broadcast_to(kf[HALF + i : HALF + i + 1], (GROUP, width)) for i in range(LAST)]
    total = jnp.zeros((GROUP, width), F32)
    for i in range(LAST):
        inner = jnp.zeros((GROUP, width), F32)
        for j in range(i + 1):
            inner = inner + jnp.concatenate([corner_ref[LAST * i + j]] * (width // HD), axis=1) * last[j]
        total = total + inner * last[i]
    return total


def logits_kernel(part, live_ref, p_ref, kt_ref, *refs):
    w_out, st_out, w_ref, mu_ref, corner_ref = refs[-5:]
    chunk, side = place(*part)
    width = kt_ref.shape[1]
    step = 256
    unpack(p_ref, w_ref, mu_ref, corner_ref)
    for s in range(0, width, step):
        kt = kt_ref[:, s : s + step]
        kf = kt.astype(F32)
        lin = jnp.dot(mu_ref[...], kt, preferred_element_type=F32)
        lin = (lin[:GROUP] + lin[GROUP : 2 * GROUP]) + lin[2 * GROUP :]
        kr = jnp.concatenate([kf[:HALF], kf[HALF + LAST :]], axis=0)
        m = jnp.dot(w_ref[...], kt, preferred_element_type=F32)
        quad = [
            jnp.sum(m[h * ROWS : (h + 1) * ROWS] * kr, axis=0, keepdims=True) for h in range(GROUP)
        ]
        quad = jnp.concatenate(quad, axis=0) + corner_sum(corner_ref, kf)
        w_out[:, s : s + step] = quad * (0.5 / HD) + lin * (1.0 / math.sqrt(HD))
    lg = w_out[...]
    live = iota(lg.shape, 1) < jnp.broadcast_to(live_ref[0:1, 0:1], lg.shape)
    peak = jnp.max(jnp.where(live, lg, -1e30), axis=1, keepdims=True)
    w = jnp.where(live, jnp.exp(jnp.where(live, lg - peak, 0.0)), 0.0)
    w_out[...] = w
    total = jnp.sum(w, axis=1, keepdims=True)
    shape = (GROUP, 2 * H)
    lane, at = iota(shape, 1), side * OWN_HEADS + chunk * GROUP + iota(shape, 0)
    both = jnp.where(lane == at, peak, 0.0) + jnp.where(lane == at + H, total, 0.0)
    st = jnp.sum(both, axis=0, keepdims=True)
    if len(refs) > 5:
        st = st + refs[0][0:1, :]
    st_out[...] = jnp.broadcast_to(st, st_out.shape)


def scores_kernel(all_ref, mine_ref, *refs):
    w_refs, vn_ref, out_ref = refs[:-2], refs[-2], refs[-1]
    every = all_ref[...]
    valid = iota(every.shape, 1) < H
    peak = jnp.max(every, axis=0, keepdims=True)
    sums = pltpu.roll(every, H, 1)
    total = jnp.where(valid, jnp.exp(jnp.where(valid, every - peak, 0.0)) * sums, 0.0)
    total = jnp.sum(total, axis=0, keepdims=True)
    ok = valid[:1]
    mine = jnp.exp(jnp.where(ok, mine_ref[0:1, :] - peak, 0.0))
    scale = jnp.where(ok, mine / jnp.where(ok, total, 1.0), 0.0)
    shape = (GROUP, 2 * H)
    width = out_ref.shape[1]

    def sums_of(w_ref, part):
        chunk, side = place(*part)
        pick = iota(shape, 1) == side * OWN_HEADS + chunk * GROUP + iota(shape, 0)
        column = jnp.sum(jnp.where(pick, scale, 0.0), axis=1, keepdims=True)
        return side * CHUNKS + chunk, jnp.sum(w_ref[...] * column, axis=0, keepdims=True)

    group = iota(out_ref.shape, 0)
    out = jnp.zeros(out_ref.shape, F32)
    for part, w_ref in zip(PARTS, w_refs):
        which, row = sums_of(w_ref, part)
        out = jnp.where(group == which, row, out)
    out_ref[...] = out * (width * DEVICES / GROUP) * vn_ref[...]


def params(mib):
    return pltpu.CompilerParams(vmem_limit_bytes=mib * 2**20)


def local(queries, query_positions, keys, cache_values, cache_length):
    n = keys.shape[0]
    nq = queries.shape[0]
    sent = pl.pallas_call(
        rotate_kernel,
        in_specs=[HBM, HBM],
        out_specs=VMEM,
        out_shape=jax.ShapeDtypeStruct((DEVICES, nq, HD), F32),
        scratch_shapes=[
            pltpu.SMEM((nq,), jnp.int32),
            pltpu.VMEM(queries.shape, BF16),
            pltpu.SemaphoreType.DMA((2,)),
        ],
        compiler_params=params(58),
        name="rotate",
    )(query_positions, queries)
    rotated = lax.all_to_all(sent, AXES, 0, 0)

    block = 1024
    turned = pl.BlockSpec((HD, block), lambda i: (0, i))
    *keys_t, vnorm, live = pl.pallas_call(
        prep_kernel,
        grid=(n // block,),
        in_specs=[SMEM] + [pl.BlockSpec((block, KVH * HD), lambda i: (i, 0))] * 2,
        out_specs=[turned] * KVH
        + [pl.BlockSpec((KVH, block), lambda i: (0, i)), pl.BlockSpec((8, HD), lambda i: (0, 0))],
        out_shape=[jax.ShapeDtypeStruct((HD, n), BF16)] * KVH
        + [jax.ShapeDtypeStruct((KVH, n), F32), jax.ShapeDtypeStruct((8, HD), jnp.int32)],
        compiler_params=params(51),
        cost_estimate=pl.CostEstimate(flops=2 * n * 512 * 512, bytes_accessed=12 * 2**20, transcendentals=0),
        name="prep",
    )(cache_length, keys, cache_values)
    rotated, keys_t, vnorm, live = lax.optimization_barrier((rotated, keys_t, vnorm, live))

    packed = pl.pallas_call(
        stats_kernel,
        in_specs=[VMEM],
        out_specs=VMEM,
        out_shape=jax.ShapeDtypeStruct((OWNERS, PACK, HD), F32),
        compiler_params=params(16),
        name="stats",
    )(rotated)
    swap = [(0, 1), (1, 0)]
    ring = [(x, (x + 1) % NX) for x in range(NX)] + [(NX + x, NX + (x - 1) % NX) for x in range(NX)]
    mine = lax.all_to_all(packed, ("z", "y"), 0, 0)
    far = lax.ppermute(mine, ("c", "x"), ring)
    stats = [mine, lax.ppermute(mine, "c", swap)]

    weights, st = [], ()
    for i, part in enumerate(PARTS):
        w, now = pl.pallas_call(
            functools.partial(logits_kernel, part),
            in_specs=[VMEM] * (3 + len(st)),
            out_specs=[VMEM, VMEM],
            out_shape=[
                jax.ShapeDtypeStruct((GROUP, n), F32),
                jax.ShapeDtypeStruct((DEVICES if i == KVH - 1 else 8, 2 * H), F32),
            ],
            scratch_shapes=[
                pltpu.VMEM((GROUP * ROWS, HD), BF16),
                pltpu.VMEM((3 * GROUP, HD), BF16),
                pltpu.VMEM((LAST * LAST, GROUP, HD), F32),
            ],
            compiler_params=params(16),
            cost_estimate=pl.CostEstimate(
                flops=2 * n * GROUP * HD * HD, bytes_accessed=2 * 2**20, transcendentals=n * GROUP
            ),
            name="logits",
        )(live, stats[i], keys_t[i], *st)
        weights.append(w)
        if i == NC - 1:
            far, now = lax.optimization_barrier((far, now))
            stats += [far, lax.ppermute(far, "c", swap)]
        st = (now,)
    every = lax.all_to_all(st[0], AXES, 0, 0)

    return pl.pallas_call(
        scores_kernel,
        in_specs=[VMEM] * (3 + KVH),
        out_specs=VMEM,
        out_shape=jax.ShapeDtypeStruct((KVH, n), F32),
        compiler_params=params(16),
        name="scores",
    )(every, st[0], *weights, vnorm)


def solution(mesh):
    fine = Mesh(mesh.devices.reshape(NZ, NY, NC, NX), AXES)
    return jax.shard_map(
        local,
        mesh=fine,
        in_specs=(P(AXES, None), P(AXES), P(AXES, None), P(AXES, None), P()),
        out_specs=P(None, AXES),
        check_vma=False,
    )
```

```python
import functools
import math

import jax
import jax.numpy as jnp
from jax import lax
from jax.experimental import pallas as pl
from jax.experimental.pallas import tpu as pltpu
from jax.sharding import Mesh
from jax.sharding import PartitionSpec as P

H = 64
KVH = 4
HD = 128
QN = 512
GROUP = H // KVH
HALF = HD // 2
AXES = ("z", "y", "c", "x")
NZ, NY, NC, NX = 4, 4, 2, 4
DEVICES = NZ * NY * NC * NX
OWNERS = NZ * NY
PLANES = OWNERS * NC
CHUNKS = H // PLANES
PACK = HALF + 8
OWN_HEADS = H // NC
LAST = 8
ROWS = HD - LAST
PARTS = ((0, 0), (0, 1), (1, 0), (1, 1))
F32 = jnp.float32
BF16 = jnp.bfloat16
VMEM = pl.BlockSpec(memory_space=pltpu.VMEM)
SMEM = pl.BlockSpec(memory_space=pltpu.SMEM)
HBM = pl.BlockSpec(memory_space=pltpu.HBM)


def iota(shape, dim):
    return lax.broadcasted_iota(jnp.int32, shape, dim)


def rotate_kernel(pos_hbm, q_hbm, out_ref, pos_ref, q_ref, sems):
    nq = q_ref.shape[0]
    pos_copy = pltpu.make_async_copy(pos_hbm, pos_ref, sems.at[0])
    q_copy = pltpu.make_async_copy(q_hbm, q_ref, sems.at[1])
    pos_copy.start()
    q_copy.start()
    query, lane = iota((nq, HD), 0), iota((nq, HD), 1)
    position = jnp.zeros((nq, HD), F32)
    pos_copy.wait()
    for i in range(nq):
        position = jnp.where(query == i, pos_ref[i].astype(F32), position)
    freqs = jnp.exp(-lax.rem(lane, HALF).astype(F32) * (2.0 * math.log(1000000.0) / HD))
    angle = position * freqs
    cos, sin = jnp.cos(angle), jnp.sin(angle)
    sin = jnp.where(lane < HALF, -sin, sin)
    q_copy.wait()
    for chunk in range(CHUNKS):
        for plane in range(PLANES):
            zy, core = divmod(plane, NC)
            head = core * OWN_HEADS + chunk * GROUP + zy
            v = q_ref[:, head * HD : (head + 1) * HD].astype(F32)
            r = v * cos + pltpu.roll(v, HALF, 1) * sin
            for x in range(chunk, NX, CHUNKS):
                out_ref[plane * NX + x] = r


def stats_kernel(r_ref, out_ref):
    half = r_ref.shape[0] // 2
    x = jnp.concatenate([r_ref[:half], r_ref[half:]], axis=1).reshape(QN, HD)
    row_h, lane_h = iota((HALF, HD), 0), iota((HALF, HD), 1)
    eye = iota((HD, HD), 0) == iota((HD, HD), 1)
    second = lax.dot_general(
        x, x, (((0,), (0,)), ((), ())), precision=lax.Precision.HIGHEST, preferred_element_type=F32
    )
    mean = jnp.sum(x, axis=0, keepdims=True) * (1.0 / QN)
    mean_col = jnp.sum(jnp.where(eye, mean, 0.0), axis=1, keepdims=True)
    sigma = second * (1.0 / QN) - mean_col * mean
    diag = jnp.sum(jnp.where(eye, sigma, 0.0), axis=0, keepdims=True)
    packed = jnp.where(row_h < lane_h, sigma[:HALF], pltpu.roll(sigma[HALF:], HALF, 1))
    row_l, lane_l = iota((LAST, HD), 0), iota((LAST, HD), 1)
    corner = jnp.zeros((LAST, HD), F32)
    for i in range(LAST):
        moved = pltpu.roll(sigma[HALF : HALF + LAST], (LAST * i - HALF) % HD, 1)
        j = lane_l - LAST * i
        moved = jnp.where(j < i, 2.0 * moved, moved)
        corner = jnp.where((row_l == i) & (j >= 0) & (j <= i), moved, corner)
    corner = jnp.sum(corner, axis=0, keepdims=True)
    tail = jnp.concatenate([mean, diag, corner, jnp.zeros((PACK - HALF - 3, HD), F32)], axis=0)
    for o in range(OWNERS):
        out_ref[o, :HALF, :] = packed
        out_ref[o, HALF:, :] = tail


def place(far, other):
    chunk, side = lax.rem(lax.axis_index("x"), CHUNKS), lax.axis_index("c")
    return (1 - chunk if far else chunk), (1 - side if other else side)


def turn_kernel(len_ref, k_ref, *refs):
    kt_refs, live_ref = refs[:-1], refs[-1]
    here = pl.num_programs(0) * k_ref.shape[0]
    live_ref[...] = jnp.full(live_ref.shape, len_ref[0] - lax.axis_index(AXES) * here, jnp.int32)
    for part, kt_ref in zip(PARTS, kt_refs):
        chunk, side = place(*part)
        low, high = k_ref[:, : CHUNKS * HD], k_ref[:, CHUNKS * HD :]
        k = jnp.where(side == 0, low, high)
        kt_ref[...] = jnp.where(chunk == 0, k[:, :HD], k[:, HD:]).T


def norms_kernel(v_ref, vn_ref):
    ones = jnp.ones((8, HD), BF16)
    nt = (((1,), (1,)), ((), ()))
    for g in range(KVH):
        v = v_ref[:, g * HD : (g + 1) * HD].astype(F32)
        sq = v * v
        hi = sq.astype(BF16)
        lo = (sq - hi.astype(F32)).astype(BF16)
        s = lax.dot_general(ones, hi, nt, preferred_element_type=F32)
        s = s + lax.dot_general(ones, lo, nt, preferred_element_type=F32)
        vn_ref[g : g + 1, :] = jnp.sqrt(s[:1] * (1.0 / HD))


def unpack(p_ref, w_ref, mu_ref, corner_ref):
    row, lane = iota((HALF, HD), 0), iota((HALF, HD), 1)
    down = lane - HALF
    means, corners, forms = [], [], []
    for h in range(GROUP):
        packed, tail = p_ref[h, :HALF, :], p_ref[h, HALF:, :]
        means.append(tail[0:1])
        diag = tail[1:2]
        corners.append(tail[2:3])
        top = jnp.where(row < lane, 2.0 * packed, jnp.where(row == lane, diag, 0.0))
        low = jnp.where(down < row, 2.0 * pltpu.roll(packed, HALF, 1), jnp.where(down == row, diag, 0.0))
        low = jnp.where(down >= 0, low, 0.0)
        forms += [top, low[LAST:]]
        if h % 2 == 1:
            w_ref[(h - 1) * ROWS : (h + 1) * ROWS, :] = jnp.concatenate(forms, axis=0).astype(BF16)
            forms = []
    mean = jnp.concatenate(means, axis=0)
    m1 = mean.astype(BF16)
    rest = mean - m1.astype(F32)
    m2 = rest.astype(BF16)
    m3 = (rest - m2.astype(F32)).astype(BF16)
    mu_ref[0:GROUP, :] = m1
    mu_ref[GROUP : 2 * GROUP, :] = m2
    mu_ref[2 * GROUP :, :] = m3
    corner = jnp.concatenate(corners, axis=0).astype(BF16).astype(F32)
    for i in range(LAST):
        for j in range(i + 1):
            at = LAST * i + j
            corner_ref[at] = jnp.broadcast_to(corner[:, at : at + 1], (GROUP, HD))


def corner_sum(corner_ref, kf):
    width = kf.shape[1]
    last = [jnp.broadcast_to(kf[HALF + i : HALF + i + 1], (GROUP, width)) for i in range(LAST)]
    total = jnp.zeros((GROUP, width), F32)
    for i in range(LAST):
        inner = jnp.zeros((GROUP, width), F32)
        for j in range(i + 1):
            inner = inner + jnp.concatenate([corner_ref[LAST * i + j]] * (width // HD), axis=1) * last[j]
        total = total + inner * last[i]
    return total


def logits_kernel(part, live_ref, p_ref, kt_ref, *refs):
    w_ref, mu_ref, corner_ref = refs[-3:]
    refs = refs[:-3]
    prev_ref, (w_out, *st_outs) = (None, refs) if part == PARTS[0] else (refs[0], refs[1:])
    chunk, side = place(*part)
    width = kt_ref.shape[1]
    step = 256
    unpack(p_ref, w_ref, mu_ref, corner_ref)
    for s in range(0, width, step):
        kt = kt_ref[:, s : s + step]
        kf = kt.astype(F32)
        lin = jnp.dot(mu_ref[...], kt, preferred_element_type=F32)
        lin = (lin[:GROUP] + lin[GROUP : 2 * GROUP]) + lin[2 * GROUP :]
        kr = jnp.concatenate([kf[:HALF], kf[HALF + LAST :]], axis=0)
        m = jnp.dot(w_ref[...], kt, preferred_element_type=F32)
        quad = [
            jnp.sum(m[h * ROWS : (h + 1) * ROWS] * kr, axis=0, keepdims=True) for h in range(GROUP)
        ]
        quad = jnp.concatenate(quad, axis=0) + corner_sum(corner_ref, kf)
        w_out[:, s : s + step] = quad * (0.5 / HD) + lin * (1.0 / math.sqrt(HD))
    lg = w_out[...]
    live = iota(lg.shape, 1) < jnp.broadcast_to(live_ref[0:1, 0:1], lg.shape)
    peak = jnp.max(jnp.where(live, lg, -1e30), axis=1, keepdims=True)
    w = jnp.where(live, jnp.exp(jnp.where(live, lg - peak, 0.0)), 0.0)
    w_out[...] = w
    total = jnp.sum(w, axis=1, keepdims=True)
    shape = (GROUP, 2 * H)
    lane, at = iota(shape, 1), side * OWN_HEADS + chunk * GROUP + iota(shape, 0)
    both = jnp.where(lane == at, peak, 0.0) + jnp.where(lane == at + H, total, 0.0)
    st = jnp.sum(both, axis=0, keepdims=True)
    if prev_ref is not None:
        st = st + prev_ref[0:1, :]
    for st_out in st_outs:
        st_out[...] = jnp.broadcast_to(st, st_out.shape)


def scores_kernel(all_ref, mine_ref, *refs):
    w_refs, vn_ref, out_ref = refs[:-2], refs[-2], refs[-1]
    every = all_ref[...]
    valid = iota(every.shape, 1) < H
    peak = jnp.max(every, axis=0, keepdims=True)
    sums = pltpu.roll(every, H, 1)
    total = jnp.where(valid, jnp.exp(jnp.where(valid, every - peak, 0.0)) * sums, 0.0)
    total = jnp.sum(total, axis=0, keepdims=True)
    ok = valid[:1]
    mine = jnp.exp(jnp.where(ok, mine_ref[0:1, :] - peak, 0.0))
    scale = jnp.where(ok, mine / jnp.where(ok, total, 1.0), 0.0)
    shape = (GROUP, 2 * H)
    width = out_ref.shape[1]

    def sums_of(w_ref, part):
        chunk, side = place(*part)
        pick = iota(shape, 1) == side * OWN_HEADS + chunk * GROUP + iota(shape, 0)
        column = jnp.sum(jnp.where(pick, scale, 0.0), axis=1, keepdims=True)
        return side * CHUNKS + chunk, jnp.sum(w_ref[...] * column, axis=0, keepdims=True)

    group = iota(out_ref.shape, 0)
    out = jnp.zeros(out_ref.shape, F32)
    for part, w_ref in zip(PARTS, w_refs):
        which, row = sums_of(w_ref, part)
        out = jnp.where(group == which, row, out)
    out_ref[...] = out * (width * DEVICES / GROUP) * vn_ref[...]


def params(mib):
    return pltpu.CompilerParams(vmem_limit_bytes=mib * 2**20)


def local(queries, query_positions, keys, cache_values, cache_length):
    n = keys.shape[0]
    nq = queries.shape[0]
    sent = pl.pallas_call(
        rotate_kernel,
        in_specs=[HBM, HBM],
        out_specs=VMEM,
        out_shape=jax.ShapeDtypeStruct((DEVICES, nq, HD), F32),
        scratch_shapes=[
            pltpu.SMEM((nq,), jnp.int32),
            pltpu.VMEM(queries.shape, BF16),
            pltpu.SemaphoreType.DMA((2,)),
        ],
        compiler_params=params(58),
        name="rotate",
    )(query_positions, queries)
    rotated = lax.all_to_all(sent, AXES, 0, 0)

    block = 1024
    rows = pl.BlockSpec((block, KVH * HD), lambda i: (i, 0))
    *keys_t, live = pl.pallas_call(
        turn_kernel,
        grid=(n // block,),
        in_specs=[SMEM, rows],
        out_specs=[pl.BlockSpec((HD, block), lambda i: (0, i))] * KVH + [pl.BlockSpec((8, HD), lambda i: (0, 0))],
        out_shape=[jax.ShapeDtypeStruct((HD, n), BF16)] * KVH + [jax.ShapeDtypeStruct((8, HD), jnp.int32)],
        compiler_params=params(51),
        cost_estimate=pl.CostEstimate(flops=2 * n * 512 * 512, bytes_accessed=8 * 2**20, transcendentals=0),
        name="turn",
    )(cache_length, keys)
    rotated, keys_t, live = lax.optimization_barrier((rotated, keys_t, live))

    packed = pl.pallas_call(
        stats_kernel,
        in_specs=[VMEM],
        out_specs=VMEM,
        out_shape=jax.ShapeDtypeStruct((OWNERS, PACK, HD), F32),
        compiler_params=params(16),
        name="stats",
    )(rotated)
    swap = [(0, 1), (1, 0)]
    ring = [(x, (x + 1) % NX) for x in range(NX)] + [(NX + x, NX + (x - 1) % NX) for x in range(NX)]
    mine = lax.all_to_all(packed, ("z", "y"), 0, 0)
    far = lax.ppermute(mine, ("c", "x"), ring)
    stats = [mine, lax.ppermute(mine, "c", swap)]

    weights, st = [], ()
    for i, part in enumerate(PARTS):
        copies = (8, DEVICES) if i == KVH - 1 else (8,)
        w, now, *wide = pl.pallas_call(
            functools.partial(logits_kernel, part),
            in_specs=[VMEM] * (3 + len(st)),
            out_specs=[VMEM] * (1 + len(copies)),
            out_shape=[jax.ShapeDtypeStruct((GROUP, n), F32)]
            + [jax.ShapeDtypeStruct((rows_out, 2 * H), F32) for rows_out in copies],
            scratch_shapes=[
                pltpu.VMEM((GROUP * ROWS, HD), BF16),
                pltpu.VMEM((3 * GROUP, HD), BF16),
                pltpu.VMEM((LAST * LAST, GROUP, HD), F32),
            ],
            compiler_params=params(16),
            cost_estimate=pl.CostEstimate(
                flops=2 * n * GROUP * HD * HD, bytes_accessed=2 * 2**20, transcendentals=n * GROUP
            ),
            name="logits",
        )(live, stats[i], keys_t[i], *st)
        weights.append(w)
        if i == NC - 1:
            far, now = lax.optimization_barrier((far, now))
            stats += [far, lax.ppermute(far, "c", swap)]
        st = (now,)
    every = lax.all_to_all(wide[0], AXES, 0, 0)
    vnorm = pl.pallas_call(
        norms_kernel,
        grid=(n // block,),
        in_specs=[rows],
        out_specs=pl.BlockSpec((KVH, block), lambda i: (0, i)),
        out_shape=jax.ShapeDtypeStruct((KVH, n), F32),
        compiler_params=params(51),
        cost_estimate=pl.CostEstimate(flops=2 * n * 512 * 512, bytes_accessed=4 * 2**20, transcendentals=0),
        name="norms",
    )(cache_values)
    every, vnorm = lax.optimization_barrier((every, vnorm))

    return pl.pallas_call(
        scores_kernel,
        in_specs=[VMEM] * (3 + KVH),
        out_specs=VMEM,
        out_shape=jax.ShapeDtypeStruct((KVH, n), F32),
        compiler_params=params(16),
        name="scores",
    )(every, st[0], *weights, vnorm)


def solution(mesh):
    fine = Mesh(mesh.devices.reshape(NZ, NY, NC, NX), AXES)
    return jax.shard_map(
        local,
        mesh=fine,
        in_specs=(P(AXES, None), P(AXES), P(AXES, None), P(AXES, None), P()),
        out_specs=P(None, AXES),
        check_vma=False,
    )
```

```python
import functools
import math

import jax
import jax.numpy as jnp
from jax import lax
from jax.experimental import pallas as pl
from jax.experimental.pallas import tpu as pltpu
from jax.sharding import Mesh
from jax.sharding import PartitionSpec as P

H = 64
KVH = 4
HD = 128
QN = 512
GROUP = H // KVH
HALF = HD // 2
AXES = ("z", "y", "c", "x")
NZ, NY, NC, NX = 4, 4, 2, 4
DEVICES = NZ * NY * NC * NX
OWNERS = NZ * NY
PLANES = OWNERS * NC
CHUNKS = H // PLANES
PACK = HALF + 8
OWN_HEADS = H // NC
LAST = 8
ROWS = HD - LAST
PARTS = ((0, 0), (0, 1), (1, 0), (1, 1))
F32 = jnp.float32
BF16 = jnp.bfloat16
VMEM = pl.BlockSpec(memory_space=pltpu.VMEM)
SMEM = pl.BlockSpec(memory_space=pltpu.SMEM)
HBM = pl.BlockSpec(memory_space=pltpu.HBM)


def iota(shape, dim):
    return lax.broadcasted_iota(jnp.int32, shape, dim)


def rotate_kernel(pos_hbm, q_hbm, out_ref, pos_ref, q_ref, sems):
    nq = q_ref.shape[0]
    pos_copy = pltpu.make_async_copy(pos_hbm, pos_ref, sems.at[0])
    q_copy = pltpu.make_async_copy(q_hbm, q_ref, sems.at[1])
    pos_copy.start()
    q_copy.start()
    query, lane = iota((nq, HD), 0), iota((nq, HD), 1)
    position = jnp.zeros((nq, HD), F32)
    pos_copy.wait()
    for i in range(nq):
        position = jnp.where(query == i, pos_ref[i].astype(F32), position)
    freqs = jnp.exp(-lax.rem(lane, HALF).astype(F32) * (2.0 * math.log(1000000.0) / HD))
    angle = position * freqs
    cos, sin = jnp.cos(angle), jnp.sin(angle)
    sin = jnp.where(lane < HALF, -sin, sin)
    q_copy.wait()
    for chunk in range(CHUNKS):
        for plane in range(PLANES):
            zy, core = divmod(plane, NC)
            head = core * OWN_HEADS + chunk * GROUP + zy
            v = q_ref[:, head * HD : (head + 1) * HD].astype(F32)
            r = v * cos + pltpu.roll(v, HALF, 1) * sin
            for x in range(chunk, NX, CHUNKS):
                out_ref[plane * NX + x] = r


def stats_kernel(r_ref, out_ref):
    half = r_ref.shape[0] // 2
    x = jnp.concatenate([r_ref[:half], r_ref[half:]], axis=1).reshape(QN, HD)
    row_h, lane_h = iota((HALF, HD), 0), iota((HALF, HD), 1)
    eye = iota((HD, HD), 0) == iota((HD, HD), 1)
    second = lax.dot_general(
        x, x, (((0,), (0,)), ((), ())), precision=lax.Precision.HIGHEST, preferred_element_type=F32
    )
    mean = jnp.sum(x, axis=0, keepdims=True) * (1.0 / QN)
    mean_col = jnp.sum(jnp.where(eye, mean, 0.0), axis=1, keepdims=True)
    sigma = second * (1.0 / QN) - mean_col * mean
    diag = jnp.sum(jnp.where(eye, sigma, 0.0), axis=0, keepdims=True)
    packed = jnp.where(row_h < lane_h, sigma[:HALF], pltpu.roll(sigma[HALF:], HALF, 1))
    row_l, lane_l = iota((LAST, HD), 0), iota((LAST, HD), 1)
    corner = jnp.zeros((LAST, HD), F32)
    for i in range(LAST):
        moved = pltpu.roll(sigma[HALF : HALF + LAST], (LAST * i - HALF) % HD, 1)
        j = lane_l - LAST * i
        moved = jnp.where(j < i, 2.0 * moved, moved)
        corner = jnp.where((row_l == i) & (j >= 0) & (j <= i), moved, corner)
    corner = jnp.sum(corner, axis=0, keepdims=True)
    tail = jnp.concatenate([mean, diag, corner, jnp.zeros((PACK - HALF - 3, HD), F32)], axis=0)
    for o in range(OWNERS):
        out_ref[o, :HALF, :] = packed
        out_ref[o, HALF:, :] = tail


def place(far, other):
    chunk, side = lax.rem(lax.axis_index("x"), CHUNKS), lax.axis_index("c")
    return (1 - chunk if far else chunk), (1 - side if other else side)


def turn_kernel(len_ref, k_ref, *refs):
    kt_refs, live_ref = refs[:-1], refs[-1]
    here = pl.num_programs(0) * k_ref.shape[0]
    live_ref[...] = jnp.full(live_ref.shape, len_ref[0] - lax.axis_index(AXES) * here, jnp.int32)
    for part, kt_ref in zip(PARTS, kt_refs):
        chunk, side = place(*part)
        low, high = k_ref[:, : CHUNKS * HD], k_ref[:, CHUNKS * HD :]
        k = jnp.where(side == 0, low, high)
        kt_ref[...] = jnp.where(chunk == 0, k[:, :HD], k[:, HD:]).T


def norms_kernel(v_ref, vn_ref):
    ones = jnp.ones((8, HD), BF16)
    nt = (((1,), (1,)), ((), ()))
    for g in range(KVH):
        v = v_ref[:, g * HD : (g + 1) * HD].astype(F32)
        sq = v * v
        hi = sq.astype(BF16)
        lo = (sq - hi.astype(F32)).astype(BF16)
        s = lax.dot_general(ones, hi, nt, preferred_element_type=F32)
        s = s + lax.dot_general(ones, lo, nt, preferred_element_type=F32)
        vn_ref[g : g + 1, :] = jnp.sqrt(s[:1] * (1.0 / HD))


def unpack(p_ref, w_ref, mu_ref, corner_ref):
    row, lane = iota((HALF, HD), 0), iota((HALF, HD), 1)
    down = lane - HALF
    means, corners, forms = [], [], []
    for h in range(GROUP):
        packed, tail = p_ref[h, :HALF, :], p_ref[h, HALF:, :]
        means.append(tail[0:1])
        diag = tail[1:2]
        corners.append(tail[2:3])
        top = jnp.where(row < lane, 2.0 * packed, jnp.where(row == lane, diag, 0.0))
        low = jnp.where(down < row, 2.0 * pltpu.roll(packed, HALF, 1), jnp.where(down == row, diag, 0.0))
        low = jnp.where(down >= 0, low, 0.0)
        forms += [top, low[LAST:]]
        if h % 2 == 1:
            w_ref[(h - 1) * ROWS : (h + 1) * ROWS, :] = jnp.concatenate(forms, axis=0).astype(BF16)
            forms = []
    mean = jnp.concatenate(means, axis=0)
    m1 = mean.astype(BF16)
    rest = mean - m1.astype(F32)
    m2 = rest.astype(BF16)
    m3 = (rest - m2.astype(F32)).astype(BF16)
    mu_ref[0:GROUP, :] = m1
    mu_ref[GROUP : 2 * GROUP, :] = m2
    mu_ref[2 * GROUP :, :] = m3
    corner = jnp.concatenate(corners, axis=0).astype(BF16).astype(F32)
    for i in range(LAST):
        for j in range(i + 1):
            at = LAST * i + j
            corner_ref[at] = jnp.broadcast_to(corner[:, at : at + 1], (GROUP, HD))


def corner_sum(corner_ref, kf):
    width = kf.shape[1]
    last = [jnp.broadcast_to(kf[HALF + i : HALF + i + 1], (GROUP, width)) for i in range(LAST)]
    total = jnp.zeros((GROUP, width), F32)
    for i in range(LAST):
        inner = jnp.zeros((GROUP, width), F32)
        for j in range(i + 1):
            inner = inner + jnp.concatenate([corner_ref[LAST * i + j]] * (width // HD), axis=1) * last[j]
        total = total + inner * last[i]
    return total


def logits_kernel(part, live_ref, p_ref, kt_ref, *refs):
    w_ref, mu_ref, corner_ref = refs[-3:]
    refs = refs[:-3]
    prev_ref, (w_out, *st_outs) = (None, refs) if part == PARTS[0] else (refs[0], refs[1:])
    chunk, side = place(*part)
    width = kt_ref.shape[1]
    step = 256
    unpack(p_ref, w_ref, mu_ref, corner_ref)
    for s in range(0, width, step):
        kt = kt_ref[:, s : s + step]
        kf = kt.astype(F32)
        lin = jnp.dot(mu_ref[...], kt, preferred_element_type=F32)
        lin = (lin[:GROUP] + lin[GROUP : 2 * GROUP]) + lin[2 * GROUP :]
        kr = jnp.concatenate([kf[:HALF], kf[HALF + LAST :]], axis=0)
        m = jnp.dot(w_ref[...], kt, preferred_element_type=F32)
        quad = [
            jnp.sum(m[h * ROWS : (h + 1) * ROWS] * kr, axis=0, keepdims=True) for h in range(GROUP)
        ]
        quad = jnp.concatenate(quad, axis=0) + corner_sum(corner_ref, kf)
        w_out[:, s : s + step] = quad * (0.5 / HD) + lin * (1.0 / math.sqrt(HD))
    lg = w_out[...]
    live = iota(lg.shape, 1) < jnp.broadcast_to(live_ref[0:1, 0:1], lg.shape)
    peak = jnp.max(jnp.where(live, lg, -1e30), axis=1, keepdims=True)
    w = jnp.where(live, jnp.exp(jnp.where(live, lg - peak, 0.0)), 0.0)
    w_out[...] = w
    total = jnp.sum(w, axis=1, keepdims=True)
    shape = (GROUP, 2 * H)
    lane, at = iota(shape, 1), side * OWN_HEADS + chunk * GROUP + iota(shape, 0)
    both = jnp.where(lane == at, peak, 0.0) + jnp.where(lane == at + H, total, 0.0)
    st = jnp.sum(both, axis=0, keepdims=True)
    if prev_ref is not None:
        st = st + prev_ref[0:1, :]
    for st_out in st_outs:
        st_out[...] = jnp.broadcast_to(st, st_out.shape)


def scores_kernel(all_ref, mine_ref, *refs):
    w_refs, vn_ref, out_ref = refs[:-2], refs[-2], refs[-1]
    every = all_ref[...]
    valid = iota(every.shape, 1) < H
    peak = jnp.max(every, axis=0, keepdims=True)
    sums = pltpu.roll(every, H, 1)
    total = jnp.where(valid, jnp.exp(jnp.where(valid, every - peak, 0.0)) * sums, 0.0)
    total = jnp.sum(total, axis=0, keepdims=True)
    ok = valid[:1]
    mine = jnp.exp(jnp.where(ok, mine_ref[0:1, :] - peak, 0.0))
    scale = jnp.where(ok, mine / jnp.where(ok, total, 1.0), 0.0)
    shape = (GROUP, 2 * H)
    width = out_ref.shape[1]

    def sums_of(w_ref, part):
        chunk, side = place(*part)
        pick = iota(shape, 1) == side * OWN_HEADS + chunk * GROUP + iota(shape, 0)
        column = jnp.sum(jnp.where(pick, scale, 0.0), axis=1, keepdims=True)
        return side * CHUNKS + chunk, jnp.sum(w_ref[...] * column, axis=0, keepdims=True)

    group = iota(out_ref.shape, 0)
    out = jnp.zeros(out_ref.shape, F32)
    for part, w_ref in zip(PARTS, w_refs):
        which, row = sums_of(w_ref, part)
        out = jnp.where(group == which, row, out)
    out_ref[...] = out * (width * DEVICES / GROUP) * vn_ref[...]


def params(mib):
    return pltpu.CompilerParams(vmem_limit_bytes=mib * 2**20)


def local(queries, query_positions, keys, cache_values, cache_length):
    n = keys.shape[0]
    nq = queries.shape[0]
    sent = pl.pallas_call(
        rotate_kernel,
        in_specs=[HBM, HBM],
        out_specs=VMEM,
        out_shape=jax.ShapeDtypeStruct((DEVICES, nq, HD), F32),
        scratch_shapes=[
            pltpu.SMEM((nq,), jnp.int32),
            pltpu.VMEM(queries.shape, BF16),
            pltpu.SemaphoreType.DMA((2,)),
        ],
        compiler_params=params(58),
        name="rotate",
    )(query_positions, queries)
    rotated = lax.all_to_all(sent, AXES, 0, 0)

    block = 1024
    rows = pl.BlockSpec((block, KVH * HD), lambda i: (i, 0))
    part = 2048
    *keys_t, live = pl.pallas_call(
        turn_kernel,
        grid=(n // part,),
        in_specs=[SMEM, pl.BlockSpec((part, KVH * HD), lambda i: (i, 0))],
        out_specs=[pl.BlockSpec((HD, part), lambda i: (0, i))] * KVH + [pl.BlockSpec((8, HD), lambda i: (0, 0))],
        out_shape=[jax.ShapeDtypeStruct((HD, n), BF16)] * KVH + [jax.ShapeDtypeStruct((8, HD), jnp.int32)],
        compiler_params=params(51),
        cost_estimate=pl.CostEstimate(flops=2 * n * 512 * 512, bytes_accessed=8 * 2**20, transcendentals=0),
        name="turn",
    )(cache_length, keys)
    rotated, keys_t, live = lax.optimization_barrier((rotated, keys_t, live))

    packed = pl.pallas_call(
        stats_kernel,
        in_specs=[VMEM],
        out_specs=VMEM,
        out_shape=jax.ShapeDtypeStruct((OWNERS, PACK, HD), F32),
        compiler_params=params(16),
        name="stats",
    )(rotated)
    swap = [(0, 1), (1, 0)]
    ring = [(x, (x + 1) % NX) for x in range(NX)] + [(NX + x, NX + (x - 1) % NX) for x in range(NX)]
    mine = lax.all_to_all(packed, ("z", "y"), 0, 0)
    far = lax.ppermute(mine, ("c", "x"), ring)
    stats = [mine, lax.ppermute(mine, "c", swap)]

    weights, st = [], ()
    for i, part in enumerate(PARTS):
        copies = (8, DEVICES) if i == KVH - 1 else (8,)
        w, now, *wide = pl.pallas_call(
            functools.partial(logits_kernel, part),
            in_specs=[VMEM] * (3 + len(st)),
            out_specs=[VMEM] * (1 + len(copies)),
            out_shape=[jax.ShapeDtypeStruct((GROUP, n), F32)]
            + [jax.ShapeDtypeStruct((rows_out, 2 * H), F32) for rows_out in copies],
            scratch_shapes=[
                pltpu.VMEM((GROUP * ROWS, HD), BF16),
                pltpu.VMEM((3 * GROUP, HD), BF16),
                pltpu.VMEM((LAST * LAST, GROUP, HD), F32),
            ],
            compiler_params=params(16),
            cost_estimate=pl.CostEstimate(
                flops=2 * n * GROUP * HD * HD, bytes_accessed=2 * 2**20, transcendentals=n * GROUP
            ),
            name="logits",
        )(live, stats[i], keys_t[i], *st)
        weights.append(w)
        if i == NC - 1:
            far, now = lax.optimization_barrier((far, now))
            stats += [far, lax.ppermute(far, "c", swap)]
        st = (now,)
    every = lax.all_to_all(wide[0], AXES, 0, 0)
    vnorm = pl.pallas_call(
        norms_kernel,
        grid=(n // block,),
        in_specs=[rows],
        out_specs=pl.BlockSpec((KVH, block), lambda i: (0, i)),
        out_shape=jax.ShapeDtypeStruct((KVH, n), F32),
        compiler_params=params(51),
        cost_estimate=pl.CostEstimate(flops=2 * n * 512 * 512, bytes_accessed=4 * 2**20, transcendentals=0),
        name="norms",
    )(cache_values)
    every, vnorm = lax.optimization_barrier((every, vnorm))

    return pl.pallas_call(
        scores_kernel,
        in_specs=[VMEM] * (3 + KVH),
        out_specs=VMEM,
        out_shape=jax.ShapeDtypeStruct((KVH, n), F32),
        compiler_params=params(16),
        name="scores",
    )(every, st[0], *weights, vnorm)


def solution(mesh):
    fine = Mesh(mesh.devices.reshape(NZ, NY, NC, NX), AXES)
    return jax.shard_map(
        local,
        mesh=fine,
        in_specs=(P(AXES, None), P(AXES), P(AXES, None), P(AXES, None), P()),
        out_specs=P(None, AXES),
        check_vma=False,
    )
```

```python
import functools
import math

import jax
import jax.numpy as jnp
from jax import lax
from jax.experimental import pallas as pl
from jax.experimental.pallas import tpu as pltpu
from jax.sharding import Mesh
from jax.sharding import PartitionSpec as P

H = 64
KVH = 4
HD = 128
QN = 512
GROUP = H // KVH
HALF = HD // 2
AXES = ("z", "y", "c", "x")
NZ, NY, NC, NX = 4, 4, 2, 4
DEVICES = NZ * NY * NC * NX
OWNERS = NZ * NY
PLANES = OWNERS * NC
CHUNKS = H // PLANES
PACK = HALF + 8
OWN_HEADS = H // NC
LAST = 8
ROWS = HD - LAST
PARTS = ((0, 0), (0, 1), (1, 0), (1, 1))
F32 = jnp.float32
BF16 = jnp.bfloat16
VMEM = pl.BlockSpec(memory_space=pltpu.VMEM)
SMEM = pl.BlockSpec(memory_space=pltpu.SMEM)
HBM = pl.BlockSpec(memory_space=pltpu.HBM)


def iota(shape, dim):
    return lax.broadcasted_iota(jnp.int32, shape, dim)


def rotate_kernel(pos_hbm, q_hbm, out_ref, pos_ref, q_ref, sems):
    nq = q_ref.shape[0]
    pos_copy = pltpu.make_async_copy(pos_hbm, pos_ref, sems.at[0])
    q_copy = pltpu.make_async_copy(q_hbm, q_ref, sems.at[1])
    pos_copy.start()
    q_copy.start()
    query, lane = iota((nq, HD), 0), iota((nq, HD), 1)
    position = jnp.zeros((nq, HD), F32)
    pos_copy.wait()
    for i in range(nq):
        position = jnp.where(query == i, pos_ref[i].astype(F32), position)
    freqs = jnp.exp(-lax.rem(lane, HALF).astype(F32) * (2.0 * math.log(1000000.0) / HD))
    angle = position * freqs
    cos, sin = jnp.cos(angle), jnp.sin(angle)
    sin = jnp.where(lane < HALF, -sin, sin)
    q_copy.wait()
    for chunk in range(CHUNKS):
        for plane in range(PLANES):
            zy, core = divmod(plane, NC)
            head = core * OWN_HEADS + chunk * GROUP + zy
            v = q_ref[:, head * HD : (head + 1) * HD].astype(F32)
            r = v * cos + pltpu.roll(v, HALF, 1) * sin
            for x in range(chunk, NX, CHUNKS):
                out_ref[plane * NX + x] = r


def stats_kernel(r_ref, out_ref):
    half = r_ref.shape[0] // 2
    x = jnp.concatenate([r_ref[:half], r_ref[half:]], axis=1).reshape(QN, HD)
    row_h, lane_h = iota((HALF, HD), 0), iota((HALF, HD), 1)
    eye = iota((HD, HD), 0) == iota((HD, HD), 1)
    second = lax.dot_general(
        x, x, (((0,), (0,)), ((), ())), precision=lax.Precision.HIGHEST, preferred_element_type=F32
    )
    mean = jnp.sum(x, axis=0, keepdims=True) * (1.0 / QN)
    mean_col = jnp.sum(jnp.where(eye, mean, 0.0), axis=1, keepdims=True)
    sigma = second * (1.0 / QN) - mean_col * mean
    diag = jnp.sum(jnp.where(eye, sigma, 0.0), axis=0, keepdims=True)
    packed = jnp.where(row_h < lane_h, sigma[:HALF], pltpu.roll(sigma[HALF:], HALF, 1))
    row_l, lane_l = iota((LAST, HD), 0), iota((LAST, HD), 1)
    corner = jnp.zeros((LAST, HD), F32)
    for i in range(LAST):
        moved = pltpu.roll(sigma[HALF : HALF + LAST], (LAST * i - HALF) % HD, 1)
        j = lane_l - LAST * i
        moved = jnp.where(j < i, 2.0 * moved, moved)
        corner = jnp.where((row_l == i) & (j >= 0) & (j <= i), moved, corner)
    corner = jnp.sum(corner, axis=0, keepdims=True)
    tail = jnp.concatenate([mean, diag, corner, jnp.zeros((PACK - HALF - 3, HD), F32)], axis=0)
    for o in range(OWNERS):
        out_ref[o, :HALF, :] = packed
        out_ref[o, HALF:, :] = tail


def place(far, other):
    chunk, side = lax.rem(lax.axis_index("x"), CHUNKS), lax.axis_index("c")
    return (1 - chunk if far else chunk), (1 - side if other else side)


def turn_kernel(k_ref, *kt_refs):
    for part, kt_ref in zip(PARTS, kt_refs):
        chunk, side = place(*part)
        low, high = k_ref[:, : CHUNKS * HD], k_ref[:, CHUNKS * HD :]
        k = jnp.where(side == 0, low, high)
        kt_ref[...] = jnp.where(chunk == 0, k[:, :HD], k[:, HD:]).T


def norms_kernel(v_ref, vn_ref):
    ones = jnp.ones((8, HD), BF16)
    nt = (((1,), (1,)), ((), ()))
    for g in range(KVH):
        v = v_ref[:, g * HD : (g + 1) * HD].astype(F32)
        sq = v * v
        hi = sq.astype(BF16)
        lo = (sq - hi.astype(F32)).astype(BF16)
        s = lax.dot_general(ones, hi, nt, preferred_element_type=F32)
        s = s + lax.dot_general(ones, lo, nt, preferred_element_type=F32)
        vn_ref[g : g + 1, :] = jnp.sqrt(s[:1] * (1.0 / HD))


def unpack(p_ref, w_ref, mu_ref, corner_ref):
    row, lane = iota((HALF, HD), 0), iota((HALF, HD), 1)
    down = lane - HALF
    means, corners, forms = [], [], []
    for h in range(GROUP):
        packed, tail = p_ref[h, :HALF, :], p_ref[h, HALF:, :]
        means.append(tail[0:1])
        diag = tail[1:2]
        corners.append(tail[2:3])
        top = jnp.where(row < lane, 2.0 * packed, jnp.where(row == lane, diag, 0.0))
        low = jnp.where(down < row, 2.0 * pltpu.roll(packed, HALF, 1), jnp.where(down == row, diag, 0.0))
        low = jnp.where(down >= 0, low, 0.0)
        forms += [top, low[LAST:]]
        if h % 2 == 1:
            w_ref[(h - 1) * ROWS : (h + 1) * ROWS, :] = jnp.concatenate(forms, axis=0).astype(BF16)
            forms = []
    mean = jnp.concatenate(means, axis=0)
    m1 = mean.astype(BF16)
    rest = mean - m1.astype(F32)
    m2 = rest.astype(BF16)
    m3 = (rest - m2.astype(F32)).astype(BF16)
    mu_ref[0:GROUP, :] = m1
    mu_ref[GROUP : 2 * GROUP, :] = m2
    mu_ref[2 * GROUP :, :] = m3
    corner = jnp.concatenate(corners, axis=0).astype(BF16).astype(F32)
    for i in range(LAST):
        for j in range(i + 1):
            at = LAST * i + j
            corner_ref[at] = jnp.broadcast_to(corner[:, at : at + 1], (GROUP, HD))


def corner_sum(corner_ref, kf):
    width = kf.shape[1]
    last = [jnp.broadcast_to(kf[HALF + i : HALF + i + 1], (GROUP, width)) for i in range(LAST)]
    total = jnp.zeros((GROUP, width), F32)
    for i in range(LAST):
        inner = jnp.zeros((GROUP, width), F32)
        for j in range(i + 1):
            inner = inner + jnp.concatenate([corner_ref[LAST * i + j]] * (width // HD), axis=1) * last[j]
        total = total + inner * last[i]
    return total


def logits_kernel(part, live_ref, p_ref, kt_ref, *refs):
    w_ref, mu_ref, corner_ref = refs[-3:]
    refs = refs[:-3]
    prev_ref, (w_out, *st_outs) = (None, refs) if part == PARTS[0] else (refs[0], refs[1:])
    chunk, side = place(*part)
    width = kt_ref.shape[1]
    step = 256
    unpack(p_ref, w_ref, mu_ref, corner_ref)
    for s in range(0, width, step):
        kt = kt_ref[:, s : s + step]
        kf = kt.astype(F32)
        lin = jnp.dot(mu_ref[...], kt, preferred_element_type=F32)
        lin = (lin[:GROUP] + lin[GROUP : 2 * GROUP]) + lin[2 * GROUP :]
        kr = jnp.concatenate([kf[:HALF], kf[HALF + LAST :]], axis=0)
        m = jnp.dot(w_ref[...], kt, preferred_element_type=F32)
        quad = [
            jnp.sum(m[h * ROWS : (h + 1) * ROWS] * kr, axis=0, keepdims=True) for h in range(GROUP)
        ]
        quad = jnp.concatenate(quad, axis=0) + corner_sum(corner_ref, kf)
        w_out[:, s : s + step] = quad * (0.5 / HD) + lin * (1.0 / math.sqrt(HD))
    lg = w_out[...]
    start = lax.axis_index(AXES) * width
    live = start + iota(lg.shape, 1) < jnp.broadcast_to(live_ref[...], lg.shape)
    peak = jnp.max(jnp.where(live, lg, -1e30), axis=1, keepdims=True)
    w = jnp.where(live, jnp.exp(jnp.where(live, lg - peak, 0.0)), 0.0)
    w_out[...] = w
    total = jnp.sum(w, axis=1, keepdims=True)
    shape = (GROUP, 2 * H)
    lane, at = iota(shape, 1), side * OWN_HEADS + chunk * GROUP + iota(shape, 0)
    both = jnp.where(lane == at, peak, 0.0) + jnp.where(lane == at + H, total, 0.0)
    st = jnp.sum(both, axis=0, keepdims=True)
    if prev_ref is not None:
        st = st + prev_ref[0:1, :]
    for st_out in st_outs:
        st_out[...] = jnp.broadcast_to(st, st_out.shape)


def scores_kernel(all_ref, mine_ref, *refs):
    w_refs, vn_ref, out_ref = refs[:-2], refs[-2], refs[-1]
    every = all_ref[...]
    valid = iota(every.shape, 1) < H
    peak = jnp.max(every, axis=0, keepdims=True)
    sums = pltpu.roll(every, H, 1)
    total = jnp.where(valid, jnp.exp(jnp.where(valid, every - peak, 0.0)) * sums, 0.0)
    total = jnp.sum(total, axis=0, keepdims=True)
    ok = valid[:1]
    mine = jnp.exp(jnp.where(ok, mine_ref[0:1, :] - peak, 0.0))
    scale = jnp.where(ok, mine / jnp.where(ok, total, 1.0), 0.0)
    shape = (GROUP, 2 * H)
    width = out_ref.shape[1]

    def sums_of(w_ref, part):
        chunk, side = place(*part)
        pick = iota(shape, 1) == side * OWN_HEADS + chunk * GROUP + iota(shape, 0)
        column = jnp.sum(jnp.where(pick, scale, 0.0), axis=1, keepdims=True)
        return side * CHUNKS + chunk, jnp.sum(w_ref[...] * column, axis=0, keepdims=True)

    group = iota(out_ref.shape, 0)
    out = jnp.zeros(out_ref.shape, F32)
    for part, w_ref in zip(PARTS, w_refs):
        which, row = sums_of(w_ref, part)
        out = jnp.where(group == which, row, out)
    out_ref[...] = out * (width * DEVICES / GROUP) * vn_ref[...]


def params(mib):
    return pltpu.CompilerParams(vmem_limit_bytes=mib * 2**20)


def local(queries, query_positions, keys, cache_values, cache_length):
    n = keys.shape[0]
    nq = queries.shape[0]
    sent = pl.pallas_call(
        rotate_kernel,
        in_specs=[HBM, HBM],
        out_specs=VMEM,
        out_shape=jax.ShapeDtypeStruct((DEVICES, nq, HD), F32),
        scratch_shapes=[
            pltpu.SMEM((nq,), jnp.int32),
            pltpu.VMEM(queries.shape, BF16),
            pltpu.SemaphoreType.DMA((2,)),
        ],
        compiler_params=params(58),
        name="rotate",
    )(query_positions, queries)
    rotated = lax.all_to_all(sent, AXES, 0, 0)

    block = 1024
    rows = pl.BlockSpec((block, KVH * HD), lambda i: (i, 0))
    part = 2048
    keys_t = pl.pallas_call(
        turn_kernel,
        grid=(n // part,),
        in_specs=[pl.BlockSpec((part, KVH * HD), lambda i: (i, 0))],
        out_specs=[pl.BlockSpec((HD, part), lambda i: (0, i))] * KVH,
        out_shape=[jax.ShapeDtypeStruct((HD, n), BF16)] * KVH,
        compiler_params=params(51),
        cost_estimate=pl.CostEstimate(flops=2 * n * 512 * 512, bytes_accessed=8 * 2**20, transcendentals=0),
        name="turn",
    )(keys)
    rotated, keys_t = lax.optimization_barrier((rotated, keys_t))

    packed = pl.pallas_call(
        stats_kernel,
        in_specs=[VMEM],
        out_specs=VMEM,
        out_shape=jax.ShapeDtypeStruct((OWNERS, PACK, HD), F32),
        compiler_params=params(16),
        name="stats",
    )(rotated)
    swap = [(0, 1), (1, 0)]
    ring = [(x, (x + 1) % NX) for x in range(NX)] + [(NX + x, NX + (x - 1) % NX) for x in range(NX)]
    mine = lax.all_to_all(packed, ("z", "y"), 0, 0)
    far = lax.ppermute(mine, ("c", "x"), ring)
    stats = [mine, lax.ppermute(mine, "c", swap)]

    weights, st = [], ()
    for i, part in enumerate(PARTS):
        copies = (8, DEVICES) if i == KVH - 1 else (8,)
        w, now, *wide = pl.pallas_call(
            functools.partial(logits_kernel, part),
            in_specs=[VMEM] * (3 + len(st)),
            out_specs=[VMEM] * (1 + len(copies)),
            out_shape=[jax.ShapeDtypeStruct((GROUP, n), F32)]
            + [jax.ShapeDtypeStruct((rows_out, 2 * H), F32) for rows_out in copies],
            scratch_shapes=[
                pltpu.VMEM((GROUP * ROWS, HD), BF16),
                pltpu.VMEM((3 * GROUP, HD), BF16),
                pltpu.VMEM((LAST * LAST, GROUP, HD), F32),
            ],
            compiler_params=params(16),
            cost_estimate=pl.CostEstimate(
                flops=2 * n * GROUP * HD * HD, bytes_accessed=2 * 2**20, transcendentals=n * GROUP
            ),
            name="logits",
        )(cache_length.reshape(1, 1), stats[i], keys_t[i], *st)
        weights.append(w)
        if i == NC - 1:
            far, now = lax.optimization_barrier((far, now))
            stats += [far, lax.ppermute(far, "c", swap)]
        st = (now,)
    every = lax.all_to_all(wide[0], AXES, 0, 0)
    vnorm = pl.pallas_call(
        norms_kernel,
        grid=(n // block,),
        in_specs=[rows],
        out_specs=pl.BlockSpec((KVH, block), lambda i: (0, i)),
        out_shape=jax.ShapeDtypeStruct((KVH, n), F32),
        compiler_params=params(51),
        cost_estimate=pl.CostEstimate(flops=2 * n * 512 * 512, bytes_accessed=4 * 2**20, transcendentals=0),
        name="norms",
    )(cache_values)
    every, vnorm = lax.optimization_barrier((every, vnorm))

    return pl.pallas_call(
        scores_kernel,
        in_specs=[VMEM] * (3 + KVH),
        out_specs=VMEM,
        out_shape=jax.ShapeDtypeStruct((KVH, n), F32),
        compiler_params=params(16),
        name="scores",
    )(every, st[0], *weights, vnorm)


def solution(mesh):
    fine = Mesh(mesh.devices.reshape(NZ, NY, NC, NX), AXES)
    return jax.shard_map(
        local,
        mesh=fine,
        in_specs=(P(AXES, None), P(AXES), P(AXES, None), P(AXES, None), P()),
        out_specs=P(None, AXES),
        check_vma=False,
    )
```
